32 devices in a mesh: rows: 16 (over z, y, core), cols: 2 (over x).
Axes of the slice: x: 2, y: 2, z: 4, core: 2. Of those that a mesh axis runs over, the one named last changes fastest.
Arguments:
- users: bfloat16 [32768, 256], P('rows'), may hold values from -0.3984375 to 0.3984375
- items: bfloat16 [2, 256, 256], P('cols'), may hold values from -6 to 6
- ratings: bfloat16 [16, 2, 64, 128, 128], P('rows', 'cols'), may hold values from -6 to 6
- tile_users: int32 [16, 2, 64], P('rows', 'cols'), may hold values from 0 to 15
- tile_items: int32 [16, 2, 64], P('rows', 'cols'), may hold values from 0 to 1
- tile_count: int32 [16, 2], P('rows', 'cols'), may hold values from 16 to 64, as said below
- send_list: int32 [16, 2, 2, 1], P('rows', 'cols'), may hold values from 0 to 1
- block_target: int32 [16, 2, 2], P('rows', 'cols'), may hold values from 0 to 1
- similarity: bfloat16 [16, 2, 2, 128, 128], P('rows', 'cols'), may hold values from -6 to 6
Outputs:
- new_items: float32 [2, 256, 256], P('cols', 'rows')
The draws below stay inside these ranges and needn't reach their ends.
Inputs may be any that keep to these rules, and one draw needn't show every extreme that they name: `tile_count`: every draw has some device with all 64 slots live; the device differs from draw to draw.
All inputs are finite; a program needn't handle non-finite values.
Results may differ from the reference program's by a relative error of at most 0.00065.
Values may be sent and summed in bfloat16 or wider, within the bound.
No kernel may reach another device: no remote copies, remote signals or barrier semaphores. Data moves between devices by JAX's collectives and lax.ppermute only.
A program may use at most 64 MiB of HBM per device.

```python
import jax
import jax.numpy as jnp
from jax import lax

R = 256
TILE = 128
UT_ROW = 16
TILES_DEV = 64
SLOTS = 1
GB = 2
IC = 256
ICT = 2
NU = 32768
N_ROWS = 16
N_COLS = 2


def draw_tile_count(key, part):
    first, second, third = jax.random.split(key, 3)
    counts = jax.random.randint(first, (N_ROWS, N_COLS), TILES_DEV // 4, TILES_DEV + 1)
    row_pick = jax.random.randint(second, (), 0, N_ROWS)
    col_pick = jax.random.randint(third, (), 0, N_COLS)
    return counts.at[row_pick, col_pick].set(TILES_DEV).astype(jnp.int32)


def place_ends(result, rng, least, top_value):
    spot = [jax.random.randint(jax.random.fold_in(rng, axis), (), 0, length) for axis, length in enumerate(result.shape)]
    longest = result.shape.index(max(result.shape))
    neighbour = spot[:longest] + [(spot[longest] + 1) % result.shape[longest]] + spot[longest + 1:]
    return result.at[tuple(spot)].set(least).at[tuple(neighbour)].set(top_value)


def block_levels(key, extent, cuts, least, largest):
    gain = 1.0
    for axis_at, blocks in cuts:
        steps = jax.random.uniform(jax.random.fold_in(jax.random.fold_in(key, 6), axis_at), (blocks,), jnp.float32, least / len(cuts), largest / len(cuts))
        gain = gain * jnp.repeat(jnp.exp(steps), extent[axis_at] // blocks).reshape((-1,) + (1,) * (len(extent) - 1 - axis_at))
    return gain


def normal_values(own_key, dims, spread, limit, pieces=(), kind=jnp.bfloat16):
    result = spread * jax.random.normal(own_key, dims, jnp.float32)
    if pieces:
        result = result * block_levels(own_key, dims, pieces, -0.22, 0.18)
    return jnp.clip(result, -limit, limit).astype(kind)


def setup_inputs(seed: int = 0) -> dict:
    key_list = jax.random.split(jax.random.key(seed), 10)
    users = normal_values(key_list[0], (NU, R), 0.0625, 0.3984375, ((0, 16),))
    items = normal_values(key_list[1], (N_COLS, IC, R), 1.0, 6.0, ((0, 2),))
    ratings = normal_values(key_list[2], (N_ROWS, N_COLS, TILES_DEV, TILE, TILE), 1.0, 6.0, ((0, 16), (1, 2)))
    tile_users = place_ends(jax.random.randint(key_list[3], (N_ROWS, N_COLS, TILES_DEV), 0, UT_ROW), jax.random.fold_in(key_list[3], 1), 0, UT_ROW - 1).astype(jnp.int32)
    tile_items = place_ends(jax.random.randint(key_list[4], (N_ROWS, N_COLS, TILES_DEV), 0, ICT), jax.random.fold_in(key_list[4], 1), 0, ICT - 1).astype(jnp.int32)
    tile_count = draw_tile_count(jax.random.fold_in(key_list[9], 71), 0)
    send_list = place_ends(jax.random.randint(key_list[6], (N_ROWS, N_COLS, N_COLS, SLOTS), 0, ICT), jax.random.fold_in(key_list[6], 1), 0, ICT - 1).astype(jnp.int32)
    block_target = place_ends(jax.random.randint(key_list[7], (N_ROWS, N_COLS, GB), 0, ICT), jax.random.fold_in(key_list[7], 1), 0, ICT - 1).astype(jnp.int32)
    similarity = normal_values(key_list[8], (N_ROWS, N_COLS, GB, TILE, TILE), 1.0, 6.0, ((0, 16), (1, 2)))
    return {"users": users, "items": items, "ratings": ratings, "tile_users": tile_users, "tile_items": tile_items, "tile_count": tile_count, "send_list": send_list, "block_target": block_target, "similarity": similarity}


def reference(users, items, ratings, tile_users, tile_items, tile_count, send_list, block_target, similarity):
    ncols, icount, rank = items.shape
    tile = ratings.shape[-1]
    ntiles = icount // tile
    tiles_here = ratings.shape[2]
    slots = send_list.shape[-1]
    blocks = similarity.shape[2]
    user_tiles = users.reshape(N_ROWS, -1, tile, rank)
    item_tiles = items.reshape(ncols, ntiles, tile, rank)
    places = jnp.arange(tiles_here, dtype=jnp.int32)
    block_ids = jnp.arange(blocks, dtype=jnp.int32)
    sources = block_ids // slots
    slot_ids = block_ids % slots

    def device_step(index, grad):
        row = (index // ncols).astype(jnp.int32)
        col = (index % ncols).astype(jnp.int32)
        own_users = user_tiles[row]
        own_items = item_tiles[col]
        left = own_users[tile_users[row, col]].astype(jnp.float32)
        right = own_items[tile_items[row, col]].astype(jnp.float32)
        pred = jnp.einsum('tar,tbr->tab', left, right)
        live = (places < tile_count[row, col]).astype(jnp.float32)
        err = ((pred - ratings[row, col].astype(jnp.float32)) * live[:, None, None]).astype(jnp.bfloat16)
        part = jnp.einsum('tab,tar->tbr', err.astype(jnp.float32), left)
        local = jnp.zeros((ntiles, tile, rank), jnp.float32).at[tile_items[row, col]].add(part)
        picked = send_list[row, sources, col, slot_ids]
        panels = item_tiles[sources, picked].astype(jnp.float32)
        contrib = jnp.einsum('kab,kbr->kar', similarity[row, col].astype(jnp.float32), panels)
        local = local.at[block_target[row, col]].add(contrib)
        return grad.at[col].add(local)
    grad = lax.fori_loop(0, N_ROWS * ncols, device_step, jnp.zeros((ncols, ntiles, tile, rank), jnp.float32))
    grad = grad.reshape(ncols, icount, rank)
    meansq = jnp.mean(grad * grad)
    return items.astype(jnp.float32) - 0.5 * grad / jnp.sqrt(meansq + 1e-06)
```

```python
import functools

import jax
import jax.numpy as jnp
from jax import lax
from jax.experimental import pallas as pl
from jax.experimental.pallas import tpu as pltpu
from jax.sharding import PartitionSpec as P

F32 = jnp.float32
BF16 = jnp.bfloat16
CHUNKS = 8


def dot(a, b, dims):
    return lax.dot_general(a, b, (dims, ((), ())), preferred_element_type=F32)


def rating_kernel(
    user_idx, item_idx, count, users_hbm, items_hbm, ratings_hbm, grad_ref,
    users, items, ratings, users_t, pred, err, sem_u, sem_i, sem_r,
):
    n_tiles, tile = ratings.shape[0], ratings.shape[1]
    n_user = users.shape[0] // tile
    n_item = items.shape[0] // tile
    width = n_tiles // CHUNKS
    live = count[0]
    copy_u = pltpu.make_async_copy(users_hbm, users, sem_u)
    copy_i = pltpu.make_async_copy(items_hbm, items, sem_i)
    copy_i.start()
    copy_u.start()

    def chunk_copy(c):
        span = pl.ds(c * width, width)
        return pltpu.make_async_copy(ratings_hbm.at[span], ratings.at[span], sem_r.at[c])

    for c in range(CHUNKS):
        @pl.when(c * width < live)
        def _():
            chunk_copy(c).start()

    err[...] = jnp.zeros_like(err)
    copy_i.wait()
    copy_u.wait()
    for u in range(n_user):
        rows = pl.ds(u * tile, tile)
        block = users[rows, :]
        users_t[:, rows] = block.T
        whole = dot(block, items[...], ((1,), (1,)))
        for j in range(n_item):
            pred[u * n_item + j] = whole[:, j * tile:(j + 1) * tile]

    def step(t, carry):
        place = user_idx[t] * n_item + item_idx[t]
        diff = pred[place] - ratings[t].astype(F32)
        err[place] += diff.astype(BF16).astype(F32)
        return carry

    for c in range(CHUNKS):
        @pl.when(c * width < live)
        def _():
            chunk_copy(c).wait()
            lax.fori_loop(c * width, jnp.minimum(live, (c + 1) * width), step, 0)

    for j in range(n_item):
        total = jnp.zeros((users.shape[1], tile), F32)
        for u in range(n_user):
            left = users_t[:, u * tile:(u + 1) * tile]
            whole = err[u * n_item + j]
            high = whole.astype(BF16)
            low = (whole - high.astype(F32)).astype(BF16)
            total += dot(left, high, ((1,), (0,))) + dot(left, low, ((1,), (0,)))
        grad_ref[j * tile:(j + 1) * tile, :] = total.T


def rating_part(user_idx, item_idx, count, users, items, ratings):
    n_tiles, tile, unused = ratings.shape
    n_pairs = (users.shape[0] // tile) * (items.shape[0] // tile)
    smem = pl.BlockSpec(memory_space=pltpu.SMEM)
    hbm = pl.BlockSpec(memory_space=pl.ANY)
    return pl.pallas_call(
        rating_kernel,
        name="rating_part",
        out_shape=jax.ShapeDtypeStruct(items.shape, F32),
        in_specs=[smem] * 3 + [hbm] * 3,
        out_specs=pl.BlockSpec(memory_space=pltpu.VMEM),
        scratch_shapes=[
            pltpu.VMEM(users.shape, BF16),
            pltpu.VMEM(items.shape, BF16),
            pltpu.VMEM(ratings.shape, BF16),
            pltpu.VMEM(users.shape[::-1], BF16),
            pltpu.VMEM((n_pairs, tile, tile), F32),
            pltpu.VMEM((n_pairs, tile, tile), F32),
            pltpu.SemaphoreType.DMA,
            pltpu.SemaphoreType.DMA,
            pltpu.SemaphoreType.DMA((CHUNKS,)),
        ],
        compiler_params=pltpu.CompilerParams(vmem_limit_bytes=48 * 1024 * 1024),
        cost_estimate=pl.CostEstimate(flops=4 * 10**8, bytes_accessed=4 * 10**6, transcendentals=0),
    )(user_idx, item_idx, count, users, items, ratings)


def graph_kernel(target, grad, similarity, panels, *outs):
    blocks, tile, unused = similarity.shape
    total = outs[-1]
    total[...] = grad[...]
    for k in range(blocks):
        rows = pl.ds(pl.multiple_of(target[k] * tile, tile), tile)
        total[rows, :] += dot(similarity[k], panels[k], ((1,), (0,)))
    me = lax.axis_index("rows")
    if len(outs) == 2:
        outs[0][...] = total[...]
        return
    keep, give = outs[:2]
    half, own = keep.shape[:2]
    for q in range(half):
        for core, out in ((0, keep), (1, give)):
            place = pl.multiple_of((me ^ (2 * q + core)) * own, own)
            out[q] = total[pl.ds(place, own), :]


def graph_part(target, grad, similarity, panels, out_shape):
    smem = pl.BlockSpec(memory_space=pltpu.SMEM)
    vmem = pl.BlockSpec(memory_space=pltpu.VMEM)
    return pl.pallas_call(
        graph_kernel,
        name="graph_part",
        out_shape=out_shape,
        in_specs=[smem] + [vmem] * 3,
        out_specs=jax.tree.map(lambda unused: vmem, out_shape),
        scratch_shapes=[pltpu.VMEM(grad.shape, F32)],
        compiler_params=pltpu.CompilerParams(vmem_limit_bytes=32 * 1024 * 1024),
    )(target, grad, similarity, panels)


def split_places(half, bit):
    return [q for q in range(half) if q & bit and not q & (bit - 1)]


def pack(total, payload, bit):
    half = total.shape[0]
    for q in range(half):
        payload[q] = total[q].astype(BF16)
    for n, q in enumerate(split_places(half, bit)):
        whole = total[q]
        payload[half + n] = (whole - whole.astype(BF16).astype(F32)).astype(BF16)


def unpack(received, q, bit, half):
    other = q ^ bit
    value = received[other].astype(F32)
    places = split_places(half, bit)
    if other in places:
        value = value + received[half + places.index(other)].astype(F32)
    return value


def first_kernel(keep, received, total, payload):
    total[...] = keep[...] + received[...]
    pack(total, payload, 1)


def next_kernel(bit, before, received, total, payload):
    half = total.shape[0]
    for q in range(half):
        total[q] = before[q] + unpack(received, q, bit, half)
    pack(total, payload, 2 * bit)


def last_kernel(bit, before, received, own, squares):
    half, rows, rank = before.shape
    part = jnp.zeros((8, 128), F32)
    for q in range(half):
        value = before[q] + unpack(received, q, bit, half)
        if q == 0:
            own[...] = value
        square = value * value
        for a in range(0, rows, 8):
            for b in range(0, rank, 128):
                part = part + square[a:a + 8, b:b + 128]
    squares[...] = part


def local_call(kernel, name, args, out_shape):
    vmem = pl.BlockSpec(memory_space=pltpu.VMEM)
    return pl.pallas_call(
        kernel, name=name, out_shape=out_shape, in_specs=[vmem] * len(args),
        out_specs=jax.tree.map(lambda unused: vmem, out_shape),
    )(*args)


def update_kernel(entries, items, own, squares, more, new):
    me = lax.axis_index("rows")
    rows = own.shape[0]
    meansq = jnp.sum(squares[...] + more[...], keepdims=True) / entries
    mine = items[pl.ds(pl.multiple_of(me * rows, rows), rows), :].astype(F32)
    new[...] = mine - 0.5 * own[...] / jnp.sqrt(meansq + 1e-06)


def swap(value, axis, bit):
    size = lax.axis_size(axis)
    return lax.ppermute(value, axis, [(i, i ^ bit) for i in range(size)])


def shards(
    users, items, ratings, tile_users, tile_items, tile_count, send_list, block_target, similarity
):
    n_rows, n_cols = lax.axis_size("rows"), lax.axis_size("cols")
    icount, rank = items.shape[1:]
    tile = ratings.shape[-1]
    blocks = similarity.shape[2]
    panels = items[0].reshape(-1, tile, rank)
    incoming = lax.all_to_all(panels[send_list[0, 0]], "cols", 0, 0, tiled=True)
    incoming = incoming.reshape(blocks, tile, rank)
    grad = rating_part(
        tile_users[0, 0], tile_items[0, 0], tile_count[0], users, items[0], ratings[0, 0]
    )
    own_rows = icount // n_rows
    entries = n_cols * icount * rank
    target = block_target[0, 0]
    if n_rows & (n_rows - 1) or n_rows < 4 or n_cols != 2 or own_rows % 16:
        flat = graph_part(target, grad, similarity[0, 0], incoming, (jax.ShapeDtypeStruct((icount, rank), F32),))[0]
        owned = lax.psum_scatter(flat, "rows", scatter_dimension=0, tiled=True)
        squares = lax.psum(jnp.sum(owned * owned), ("rows", "cols"))
        mine = lax.dynamic_slice_in_dim(items[0], lax.axis_index("rows") * own_rows, own_rows, 0)
        return (mine.astype(F32) - 0.5 * owned / jnp.sqrt(squares / entries + 1e-06))[None]

    half = n_rows // 2
    block = jax.ShapeDtypeStruct((half, own_rows, rank), F32)

    def payload(bit):
        return jax.ShapeDtypeStruct((half + len(split_places(half, bit)), own_rows, rank), BF16)

    keep, give = graph_part(target, grad, similarity[0, 0], incoming, (block, block))
    total, sent = local_call(first_kernel, "add_core", (keep, swap(give, "rows", 1)), (block, payload(1)))
    bit = 1
    while 2 * bit < half:
        received = swap(sent, "rows", 2 * bit)
        total, sent = local_call(
            functools.partial(next_kernel, bit), "add_" + str(bit), (total, received), (block, payload(2 * bit))
        )
        bit *= 2
    own, squares = local_call(
        functools.partial(last_kernel, bit), "add_last", (total, swap(sent, "rows", 2 * bit)),
        (jax.ShapeDtypeStruct((own_rows, rank), F32), jax.ShapeDtypeStruct((8, 128), F32)),
    )
    squares = squares + swap(squares, "rows", 1)
    updated = local_call(
        functools.partial(update_kernel, entries), "update", (items[0], own, squares, swap(squares, "cols", 1)),
        jax.ShapeDtypeStruct((own_rows, rank), F32),
    )
    return updated[None]


def solution(mesh):
    in_specs = (
        P("rows", None),
        P("cols", None, None),
        P("rows", "cols", None, None, None),
        P("rows", "cols", None),
        P("rows", "cols", None),
        P("rows", "cols"),
        P("rows", "cols", None, None),
        P("rows", "cols", None),
        P("rows", "cols", None, None, None),
    )
    out_specs = P("cols", "rows", None)
    return jax.shard_map(shards, mesh=mesh, in_specs=in_specs, out_specs=out_specs, check_vma=False)
```

```python
import functools

import jax
import jax.numpy as jnp
from jax import lax
from jax.experimental import pallas as pl
from jax.experimental.pallas import tpu as pltpu
from jax.sharding import PartitionSpec as P

F32 = jnp.float32
BF16 = jnp.bfloat16
CHUNKS = 8
SMALL = 4 * 1024 * 1024


def in_hbm(*arrays):
    return [pltpu.with_memory_space_constraint(a, pltpu.HBM) for a in arrays]


def dot(a, b, dims):
    return lax.dot_general(a, b, (dims, ((), ())), preferred_element_type=F32)


def rating_kernel(
    user_idx_hbm, item_idx_hbm, count_hbm, users_hbm, items_hbm, ratings_hbm, grad_ref, mine_ref,
    user_idx, item_idx, count, users, items, ratings, users_t, pred, err, sem_s, sem_u, sem_i, sem_r,
):
    n_tiles, tile = ratings.shape[0], ratings.shape[1]
    n_user = users.shape[0] // tile
    n_item = items.shape[0] // tile
    width = n_tiles // CHUNKS
    scalars = [
        pltpu.make_async_copy(source, target, sem_s.at[n])
        for n, (source, target) in enumerate(((count_hbm, count), (user_idx_hbm, user_idx), (item_idx_hbm, item_idx)))
    ]
    for copy in scalars:
        copy.start()
    copy_u = pltpu.make_async_copy(users_hbm, users, sem_u)
    copy_i = pltpu.make_async_copy(items_hbm, items, sem_i)
    copy_i.start()
    copy_u.start()
    for copy in scalars:
        copy.wait()
    live = count[0]

    def chunk_copy(c):
        span = pl.ds(c * width, width)
        return pltpu.make_async_copy(ratings_hbm.at[span], ratings.at[span], sem_r.at[c])

    for c in range(CHUNKS):
        @pl.when(c * width < live)
        def _():
            chunk_copy(c).start()

    err[...] = jnp.zeros_like(err)
    copy_i.wait()
    rows = mine_ref.shape[0]
    mine_ref[...] = items[pl.ds(pl.multiple_of(lax.axis_index("rows") * rows, rows), rows), :]
    copy_u.wait()
    for u in range(n_user):
        rows = pl.ds(u * tile, tile)
        block = users[rows, :]
        users_t[:, rows] = block.T
        whole = dot(block, items[...], ((1,), (1,)))
        for j in range(n_item):
            pred[u * n_item + j] = whole[:, j * tile:(j + 1) * tile]

    def step(t, carry):
        place = user_idx[t] * n_item + item_idx[t]
        diff = pred[place] - ratings[t].astype(F32)
        err[place] += diff.astype(BF16).astype(F32)
        return carry

    for c in range(CHUNKS):
        @pl.when(c * width < live)
        def _():
            chunk_copy(c).wait()
            lax.fori_loop(c * width, jnp.minimum(live, (c + 1) * width), step, 0)

    for j in range(n_item):
        total = jnp.zeros((users.shape[1], tile), F32)
        for u in range(n_user):
            left = users_t[:, u * tile:(u + 1) * tile]
            whole = err[u * n_item + j]
            high = whole.astype(BF16)
            low = (whole - high.astype(F32)).astype(BF16)
            total += dot(left, high, ((1,), (0,))) + dot(left, low, ((1,), (0,)))
        grad_ref[j * tile:(j + 1) * tile, :] = total.T


def rating_part(user_idx, item_idx, count, users, items, ratings, own_rows):
    n_tiles, tile, unused = ratings.shape
    n_pairs = (users.shape[0] // tile) * (items.shape[0] // tile)
    hbm = pl.BlockSpec(memory_space=pltpu.HBM)
    vmem = pl.BlockSpec(memory_space=pltpu.VMEM)
    return pl.pallas_call(
        rating_kernel,
        name="rating_part",
        out_shape=(
            jax.ShapeDtypeStruct(items.shape, F32),
            jax.ShapeDtypeStruct((own_rows, items.shape[1]), BF16),
        ),
        in_specs=[hbm] * 6,
        out_specs=(vmem, vmem),
        scratch_shapes=[
            pltpu.SMEM(user_idx.shape, jnp.int32),
            pltpu.SMEM(item_idx.shape, jnp.int32),
            pltpu.SMEM(count.shape, jnp.int32),
            pltpu.VMEM(users.shape, BF16),
            pltpu.VMEM(items.shape, BF16),
            pltpu.VMEM(ratings.shape, BF16),
            pltpu.VMEM(users.shape[::-1], BF16),
            pltpu.VMEM((n_pairs, tile, tile), F32),
            pltpu.VMEM((n_pairs, tile, tile), F32),
            pltpu.SemaphoreType.DMA((3,)),
            pltpu.SemaphoreType.DMA,
            pltpu.SemaphoreType.DMA,
            pltpu.SemaphoreType.DMA((CHUNKS,)),
        ],
        compiler_params=pltpu.CompilerParams(vmem_limit_bytes=48 * 1024 * 1024),
        cost_estimate=pl.CostEstimate(flops=4 * 10**8, bytes_accessed=4 * 10**6, transcendentals=0),
    )(*in_hbm(user_idx, item_idx), count, *in_hbm(users, items, ratings))


def pick_kernel(send_list_hbm, items_hbm, kept, sent, send_list, items, sem_s, sem):
    copy_list = pltpu.make_async_copy(send_list_hbm, send_list, sem_s)
    copy = pltpu.make_async_copy(items_hbm, items, sem)
    copy_list.start()
    copy.start()
    copy_list.wait()
    copy.wait()
    tile = kept.shape[0]
    me = lax.axis_index("cols")
    for out, col in ((kept, me), (sent, 1 - me)):
        out[...] = items[pl.ds(pl.multiple_of(send_list[col] * tile, tile), tile), :]


def pick_panels(send_list, items, tile):
    panel = jax.ShapeDtypeStruct((tile, items.shape[1]), BF16)
    vmem = pl.BlockSpec(memory_space=pltpu.VMEM)
    return pl.pallas_call(
        pick_kernel,
        name="pick_panels",
        out_shape=(panel, panel),
        in_specs=[pl.BlockSpec(memory_space=pltpu.HBM)] * 2,
        out_specs=(vmem, vmem),
        scratch_shapes=[
            pltpu.SMEM(send_list.shape, jnp.int32),
            pltpu.VMEM(items.shape, BF16),
            pltpu.SemaphoreType.DMA,
            pltpu.SemaphoreType.DMA,
        ],
        compiler_params=pltpu.CompilerParams(vmem_limit_bytes=SMALL),
    )(*in_hbm(send_list, items))


def parity(value):
    return bin(value).count("1") % 2


def hops(n_rows, odd):
    bits = [1 << b for b in range(1, n_rows.bit_length() - 1)]
    return bits[1:] + bits[:1] if odd else bits


def offset(n_rows, odd, q):
    value = sum(bit for b, bit in enumerate(hops(n_rows, odd)) if q >> b & 1)
    return value | parity(value)


def graph_kernel(n_panels, target, grad, similarity, *refs):
    panels, outs, total = refs[:n_panels], refs[n_panels:-1], refs[-1]
    blocks, tile, unused = similarity.shape
    total[...] = grad[...]
    col = lax.axis_index("cols")
    for k in range(blocks):
        block = k if n_panels == 1 else k ^ col
        panel = panels[0][k] if n_panels == 1 else panels[k][...]
        rows = pl.ds(pl.multiple_of(target[block] * tile, tile), tile)
        total[rows, :] += dot(similarity[block], panel, ((1,), (0,)))
    me = lax.axis_index("rows")
    if len(outs) == 1:
        outs[0][...] = total[...]
        return
    keep, give = outs
    half, own = keep.shape[:2]
    odd = sum((me >> b) & 1 for b in range(half.bit_length())) % 2
    for q in range(half):
        even_place, odd_place = (offset(2 * half, parity_, q) for parity_ in (0, 1))
        for out, block in (
            (keep, me ^ jnp.where(odd == 1, odd_place, even_place)),
            (give, me ^ 1 ^ jnp.where(odd == 1, even_place, odd_place)),
        ):
            out[q] = total[pl.ds(pl.multiple_of(block * own, own), own), :]


def graph_part(target, grad, similarity, panels, out_shape):
    smem = pl.BlockSpec(memory_space=pltpu.SMEM)
    vmem = pl.BlockSpec(memory_space=pltpu.VMEM)
    return pl.pallas_call(
        functools.partial(graph_kernel, len(panels)),
        name="graph_part",
        out_shape=out_shape,
        in_specs=[smem] + [vmem] * (2 + len(panels)),
        out_specs=jax.tree.map(lambda unused: vmem, out_shape),
        scratch_shapes=[pltpu.VMEM(grad.shape, F32)],
        compiler_params=pltpu.CompilerParams(vmem_limit_bytes=SMALL if grad.size <= 2**16 else 32 * 1024 * 1024),
    )(target, grad, similarity, *panels)


def split_places(half, bit):
    return [q for q in range(half) if q & bit and not q & (bit - 1)]


def pack(total, payload, bit):
    half = total.shape[0]
    for q in range(half):
        payload[q] = total[q].astype(BF16)
    for n, q in enumerate(split_places(half, bit)):
        whole = total[q]
        payload[half + n] = (whole - whole.astype(BF16).astype(F32)).astype(BF16)


def unpack(received, q, bit, half):
    other = q ^ bit
    value = received[other].astype(F32)
    places = split_places(half, bit)
    if other in places:
        value = value + received[half + places.index(other)].astype(F32)
    return value


def first_kernel(keep, received, total, payload):
    total[...] = keep[...] + received[...]
    pack(total, payload, 1)


def next_kernel(bit, before, received, total, payload):
    half = total.shape[0]
    for q in range(half):
        total[q] = before[q] + unpack(received, q, bit, half)
    pack(total, payload, 2 * bit)


def last_kernel(bit, before, received, own, squares):
    half, rows, rank = before.shape
    part = jnp.zeros((8, 128), F32)
    for q in range(half):
        value = before[q] + unpack(received, q, bit, half)
        if q == 0:
            own[...] = value
        square = value * value
        for a in range(0, rows, 8):
            for b in range(0, rank, 128):
                part = part + square[a:a + 8, b:b + 128]
    squares[...] = part


def local_call(kernel, name, args, out_shape):
    vmem = pl.BlockSpec(memory_space=pltpu.VMEM)
    return pl.pallas_call(
        kernel, name=name, out_shape=out_shape, in_specs=[vmem] * len(args),
        out_specs=jax.tree.map(lambda unused: vmem, out_shape),
        compiler_params=pltpu.CompilerParams(vmem_limit_bytes=SMALL),
    )(*args)


def update_kernel(entries, mine, own, squares, more, new):
    meansq = jnp.sum(squares[...] + more[...], keepdims=True) / entries
    new[...] = mine[...].astype(F32) - 0.5 * own[...] / jnp.sqrt(meansq + 1e-06)


def swap(value, axis, bit):
    size = lax.axis_size(axis)
    return lax.ppermute(value, axis, [(i, i ^ bit) for i in range(size)])


def hop(value, b):
    size = lax.axis_size("rows")
    return lax.ppermute(value, "rows", [(i, i ^ 1 ^ hops(size, parity(i))[b]) for i in range(size)])


def shards(
    users, items, ratings, tile_users, tile_items, tile_count, send_list, block_target, similarity
):
    n_rows, n_cols = lax.axis_size("rows"), lax.axis_size("cols")
    icount, rank = items.shape[1:]
    tile = ratings.shape[-1]
    blocks = similarity.shape[2]
    panels = items[0].reshape(-1, tile, rank)
    slots = send_list.shape[3]
    if n_cols == 2 and slots == 1:
        kept, sent = pick_panels(send_list.reshape(-1), items[0], tile)
        incoming = (kept, swap(sent, "cols", 1))
    else:
        incoming = lax.all_to_all(panels[send_list[0, 0]], "cols", 0, 0, tiled=True)
        incoming = (incoming.reshape(blocks, tile, rank),)
    own_rows = icount // n_rows
    grad, mine = rating_part(
        tile_users.reshape(-1), tile_items.reshape(-1), tile_count.reshape(-1), users, items[0], ratings[0, 0], own_rows
    )
    entries = n_cols * icount * rank
    target = block_target[0, 0]
    if n_rows & (n_rows - 1) or n_rows < 4 or n_cols != 2 or own_rows % 16:
        flat = graph_part(target, grad, similarity[0, 0], incoming, (jax.ShapeDtypeStruct((icount, rank), F32),))[0]
        owned = lax.psum_scatter(flat, "rows", scatter_dimension=0, tiled=True)
        squares = lax.psum(jnp.sum(owned * owned), ("rows", "cols"))
        return (mine.astype(F32) - 0.5 * owned / jnp.sqrt(squares / entries + 1e-06))[None]

    half = n_rows // 2
    block = jax.ShapeDtypeStruct((half, own_rows, rank), F32)

    def payload(bit):
        return jax.ShapeDtypeStruct((half + len(split_places(half, bit)), own_rows, rank), BF16)

    keep, give = graph_part(target, grad, similarity[0, 0], incoming, (block, block))
    total, sent = local_call(first_kernel, "add_core", (keep, swap(give, "rows", 1)), (block, payload(1)))
    n_hops = len(hops(n_rows, 0))
    for b in range(n_hops - 1):
        total, sent = local_call(
            functools.partial(next_kernel, 1 << b), "add_" + str(b), (total, hop(sent, b)), (block, payload(2 << b))
        )
    own, squares = local_call(
        functools.partial(last_kernel, half // 2), "add_last", (total, hop(sent, n_hops - 1)),
        (jax.ShapeDtypeStruct((own_rows, rank), F32), jax.ShapeDtypeStruct((8, 128), F32)),
    )
    squares = squares + swap(squares, "rows", 1)
    updated = local_call(
        functools.partial(update_kernel, entries), "update", (mine, own, squares, swap(squares, ("rows", "cols"), 3)),
        jax.ShapeDtypeStruct((own_rows, rank), F32),
    )
    return updated[None]


def solution(mesh):
    in_specs = (
        P("rows", None),
        P("cols", None, None),
        P("rows", "cols", None, None, None),
        P("rows", "cols", None),
        P("rows", "cols", None),
        P("rows", "cols"),
        P("rows", "cols", None, None),
        P("rows", "cols", None),
        P("rows", "cols", None, None, None),
    )
    out_specs = P("cols", "rows", None)
    return jax.shard_map(shards, mesh=mesh, in_specs=in_specs, out_specs=out_specs, check_vma=False)
```

```python
import functools

import jax
import jax.numpy as jnp
from jax import lax
from jax.experimental import pallas as pl
from jax.experimental.pallas import tpu as pltpu
from jax.sharding import PartitionSpec as P

F32 = jnp.float32
BF16 = jnp.bfloat16
UNROLL = 4
SMALL = 4 * 1024 * 1024


def in_hbm(*arrays):
    return [pltpu.with_memory_space_constraint(a, pltpu.HBM) for a in arrays]


def dot(a, b, dims):
    return lax.dot_general(a, b, (dims, ((), ())), preferred_element_type=F32)


def rating_kernel(
    user_idx_hbm, item_idx_hbm, target_hbm, count, users, items, ratings, grad_ref, mine_ref, hit_ref,
    user_idx, item_idx, target, items_t, pred, err, sem_s,
):
    n_tiles, tile = ratings.shape[0], ratings.shape[1]
    n_item = items.shape[0] // tile
    scalars = [
        pltpu.make_async_copy(source, target, sem_s.at[n])
        for n, (source, target) in enumerate(((target_hbm, target), (user_idx_hbm, user_idx), (item_idx_hbm, item_idx)))
    ]
    for copy in scalars:
        copy.start()
    own = mine_ref.shape[0]
    mine_ref[...] = items[pl.ds(pl.multiple_of(lax.axis_index("rows") * own, own), own), :]
    for j in range(n_item):
        items_t[j] = items[j * tile:(j + 1) * tile, :].T
    for first in range(0, n_item, 2):
        both = range(first, min(first + 2, n_item))
        whole = dot(users[...], jnp.concatenate([items_t[j] for j in both], axis=1), ((1,), (0,)))
        for n, j in enumerate(both):
            pred[j] = whole[:, n * tile:(n + 1) * tile]

    @pl.loop(0, users.shape[0] // tile)
    def _(c):
        for j in range(n_item):
            err[j, pl.ds(pl.multiple_of(c * tile, tile), tile), :] = jnp.zeros((tile, tile), F32)

    for copy in scalars:
        copy.wait()
    live = count[0, 0]
    for k in range(hit_ref.shape[0]):
        for j in range(n_item):
            hit_ref[k, j] = jnp.full((8, 128), (target[k] == j).astype(F32))

    def add_tile(t):
        j = item_idx[t]
        rows = pl.ds(pl.multiple_of(user_idx[t] * tile, tile), tile)
        diff = pred[j, rows, :] - ratings[t].astype(F32)
        err[j, rows, :] += diff.astype(BF16).astype(F32)

    groups = lax.div(live, UNROLL)

    @pl.loop(0, groups)
    def _(g):
        for k in range(UNROLL):
            add_tile(g * UNROLL + k)

    @pl.loop(groups * UNROLL, live)
    def _(t):
        add_tile(t)

    for j in range(n_item):
        whole = err[j]
        high = whole.astype(BF16)
        low = (whole - high.astype(F32)).astype(BF16)
        grad_ref[j * tile:(j + 1) * tile, :] = dot(high, users[...], ((0,), (0,))) + dot(low, users[...], ((0,), (0,)))


def rating_part(user_idx, item_idx, count, target, users, items, ratings, own_rows):
    tile = ratings.shape[1]
    n_item = items.shape[0] // tile
    smem = pl.BlockSpec(memory_space=pltpu.SMEM)
    hbm = pl.BlockSpec(memory_space=pltpu.HBM)
    vmem = pl.BlockSpec(memory_space=pltpu.VMEM)
    sums = pltpu.VMEM((n_item, users.shape[0], tile), F32)
    limit = 16 if n_item <= 2 else 56
    return pl.pallas_call(
        rating_kernel,
        name="rating_part",
        out_shape=(
            jax.ShapeDtypeStruct(items.shape, F32),
            jax.ShapeDtypeStruct((own_rows, items.shape[1]), BF16),
            jax.ShapeDtypeStruct((target.shape[0], n_item, 8, 128), F32),
        ),
        in_specs=[hbm] * 3 + [smem] + [vmem] * 3,
        out_specs=(vmem, vmem, vmem),
        scratch_shapes=[
            pltpu.SMEM(user_idx.shape, jnp.int32),
            pltpu.SMEM(item_idx.shape, jnp.int32),
            pltpu.SMEM(target.shape, jnp.int32),
            pltpu.VMEM((n_item, items.shape[1], tile), BF16),
            sums,
            sums,
            pltpu.SemaphoreType.DMA((3,)),
        ],
        compiler_params=pltpu.CompilerParams(vmem_limit_bytes=limit * 1024 * 1024),
    )(*in_hbm(user_idx, item_idx, target), count, users, items, ratings)


def pick_kernel(send_list_hbm, items_hbm, kept, sent, send_list, items, sem_s, sem):
    copy_list = pltpu.make_async_copy(send_list_hbm, send_list, sem_s)
    copy = pltpu.make_async_copy(items_hbm, items, sem)
    copy_list.start()
    copy.start()
    copy_list.wait()
    copy.wait()
    tile = kept.shape[0]
    me = lax.axis_index("cols")
    for out, col in ((kept, me), (sent, 1 - me)):
        out[...] = items[pl.ds(pl.multiple_of(send_list[col] * tile, tile), tile), :]


def pick_panels(send_list, items, tile):
    panel = jax.ShapeDtypeStruct((tile, items.shape[1]), BF16)
    vmem = pl.BlockSpec(memory_space=pltpu.VMEM)
    return pl.pallas_call(
        pick_kernel,
        name="pick_panels",
        out_shape=(panel, panel),
        in_specs=[pl.BlockSpec(memory_space=pltpu.HBM)] * 2,
        out_specs=(vmem, vmem),
        scratch_shapes=[
            pltpu.SMEM(send_list.shape, jnp.int32),
            pltpu.VMEM(items.shape, BF16),
            pltpu.SemaphoreType.DMA,
            pltpu.SemaphoreType.DMA,
        ],
        compiler_params=pltpu.CompilerParams(vmem_limit_bytes=SMALL),
        cost_estimate=pl.CostEstimate(flops=10**10, bytes_accessed=3 * 10**7, transcendentals=0),
    )(*in_hbm(send_list, items))


def parity(value):
    return bin(value).count("1") % 2


def hops(n_rows, odd):
    bits = [1 << b for b in range(1, n_rows.bit_length() - 1)]
    return bits[1:] + bits[:1] if odd else bits


def offset(n_rows, odd, q):
    value = sum(bit for b, bit in enumerate(hops(n_rows, odd)) if q >> b & 1)
    return value | parity(value)


def graph_kernel(n_panels, hit, grad, similarity, *refs):
    panels, outs, total = refs[:n_panels], refs[n_panels:-1], refs[-1]
    blocks, tile, unused = similarity.shape
    total[...] = grad[...]
    col = lax.axis_index("cols")
    for k in range(blocks):
        block = k if n_panels == 1 else k ^ col
        panel = panels[0][k] if n_panels == 1 else panels[k][...]
        part = dot(similarity[block], panel, ((1,), (0,)))
        for j in range(total.shape[0] // tile):
            chosen = jnp.broadcast_to(hit[block, j][:1, :1], part.shape) > 0
            total[j * tile:(j + 1) * tile, :] += jnp.where(chosen, part, 0)
    me = lax.axis_index("rows")
    if len(outs) == 1:
        outs[0][...] = total[...]
        return
    keep, give = outs
    half, own = keep.shape[:2]
    odd = sum((me >> b) & 1 for b in range(half.bit_length())) % 2
    for q in range(half):
        even_place, odd_place = (offset(2 * half, parity_, q) for parity_ in (0, 1))
        for out, block in (
            (keep, me ^ jnp.where(odd == 1, odd_place, even_place)),
            (give, me ^ 1 ^ jnp.where(odd == 1, even_place, odd_place)),
        ):
            out[q] = total[pl.ds(pl.multiple_of(block * own, own), own), :]


def graph_part(hit, grad, similarity, panels, out_shape):
    vmem = pl.BlockSpec(memory_space=pltpu.VMEM)
    return pl.pallas_call(
        functools.partial(graph_kernel, len(panels)),
        name="graph_part",
        out_shape=out_shape,
        in_specs=[vmem] * (3 + len(panels)),
        out_specs=jax.tree.map(lambda unused: vmem, out_shape),
        scratch_shapes=[pltpu.VMEM(grad.shape, F32)],
        compiler_params=pltpu.CompilerParams(vmem_limit_bytes=SMALL if grad.size <= 2**16 else 32 * 1024 * 1024),
    )(hit, grad, similarity, *panels)


def split_places(half, bit):
    return [q for q in range(half) if q & bit and not q & (bit - 1)]


def pack(total, payload, bit):
    half = total.shape[0]
    for q in range(half):
        payload[q] = total[q].astype(BF16)
    for n, q in enumerate(split_places(half, bit)):
        whole = total[q]
        payload[half + n] = (whole - whole.astype(BF16).astype(F32)).astype(BF16)


def unpack(received, q, bit, half):
    other = q ^ bit
    value = received[other].astype(F32)
    places = split_places(half, bit)
    if other in places:
        value = value + received[half + places.index(other)].astype(F32)
    return value


def first_kernel(keep, received, total, payload):
    total[...] = keep[...] + received[...]
    pack(total, payload, 1)


def next_kernel(bit, before, received, total, payload):
    half = total.shape[0]
    for q in range(half):
        total[q] = before[q] + unpack(received, q, bit, half)
    pack(total, payload, 2 * bit)


def last_kernel(bit, before, received, own, squares):
    half, rows, rank = before.shape
    part = jnp.zeros((8, 128), F32)
    for q in range(half):
        value = before[q] + unpack(received, q, bit, half)
        if q == 0:
            own[...] = value
        square = value * value
        for a in range(0, rows, 8):
            for b in range(0, rank, 128):
                part = part + square[a:a + 8, b:b + 128]
    squares[...] = part


def local_call(kernel, name, args, out_shape):
    vmem = pl.BlockSpec(memory_space=pltpu.VMEM)
    return pl.pallas_call(
        kernel, name=name, out_shape=out_shape, in_specs=[vmem] * len(args),
        out_specs=jax.tree.map(lambda unused: vmem, out_shape),
        compiler_params=pltpu.CompilerParams(vmem_limit_bytes=SMALL),
    )(*args)


def update_kernel(entries, mine, own, squares, more, new):
    meansq = jnp.sum(squares[...] + more[...], keepdims=True) / entries
    new[...] = mine[...].astype(F32) - 0.5 * own[...] / jnp.sqrt(meansq + 1e-06)


def swap(value, axis, bit):
    size = lax.axis_size(axis)
    return lax.ppermute(value, axis, [(i, i ^ bit) for i in range(size)])


def hop(value, b):
    size = lax.axis_size("rows")
    return lax.ppermute(value, "rows", [(i, i ^ 1 ^ hops(size, parity(i))[b]) for i in range(size)])


def shards(
    users, items, ratings, tile_users, tile_items, tile_count, send_list, block_target, similarity
):
    n_rows, n_cols = lax.axis_size("rows"), lax.axis_size("cols")
    icount, rank = items.shape[1:]
    tile = ratings.shape[-1]
    blocks = similarity.shape[2]
    panels = items[0].reshape(-1, tile, rank)
    slots = send_list.shape[3]
    if n_cols == 2 and slots == 1:
        kept, sent = pick_panels(send_list.reshape(-1), items[0], tile)
        incoming = (kept, swap(sent, "cols", 1))
    else:
        incoming = lax.all_to_all(panels[send_list[0, 0]], "cols", 0, 0, tiled=True)
        incoming = (incoming.reshape(blocks, tile, rank),)
    own_rows = icount // n_rows
    target = block_target.reshape(-1)
    grad, mine, hit = rating_part(
        tile_users.reshape(-1), tile_items.reshape(-1), tile_count, target, users, items[0],
        ratings[0, 0], own_rows,
    )
    entries = n_cols * icount * rank
    if n_rows & (n_rows - 1) or n_rows < 4 or n_cols != 2 or own_rows % 16:
        flat = graph_part(hit, grad, similarity[0, 0], incoming, (jax.ShapeDtypeStruct((icount, rank), F32),))[0]
        owned = lax.psum_scatter(flat, "rows", scatter_dimension=0, tiled=True)
        squares = lax.psum(jnp.sum(owned * owned), ("rows", "cols"))
        return (mine.astype(F32) - 0.5 * owned / jnp.sqrt(squares / entries + 1e-06))[None]

    half = n_rows // 2
    block = jax.ShapeDtypeStruct((half, own_rows, rank), F32)

    def payload(bit):
        return jax.ShapeDtypeStruct((half + len(split_places(half, bit)), own_rows, rank), BF16)

    keep, give = graph_part(hit, grad, similarity[0, 0], incoming, (block, block))
    total, sent = local_call(first_kernel, "add_core", (keep, swap(give, "rows", 1)), (block, payload(1)))
    n_hops = len(hops(n_rows, 0))
    for b in range(n_hops - 1):
        total, sent = local_call(
            functools.partial(next_kernel, 1 << b), "add_" + str(b), (total, hop(sent, b)), (block, payload(2 << b))
        )
    own, squares = local_call(
        functools.partial(last_kernel, half // 2), "add_last", (total, hop(sent, n_hops - 1)),
        (jax.ShapeDtypeStruct((own_rows, rank), F32), jax.ShapeDtypeStruct((8, 128), F32)),
    )
    squares = squares + swap(squares, "rows", 1)
    updated = local_call(
        functools.partial(update_kernel, entries), "update", (mine, own, squares, swap(squares, ("rows", "cols"), 3)),
        jax.ShapeDtypeStruct((own_rows, rank), F32),
    )
    return updated[None]


def solution(mesh):
    in_specs = (
        P("rows", None),
        P("cols", None, None),
        P("rows", "cols", None, None, None),
        P("rows", "cols", None),
        P("rows", "cols", None),
        P("rows", "cols"),
        P("rows", "cols", None, None),
        P("rows", "cols", None),
        P("rows", "cols", None, None, None),
    )
    out_specs = P("cols", "rows", None)
    return jax.shard_map(shards, mesh=mesh, in_specs=in_specs, out_specs=out_specs, check_vma=False)
```

```python
import functools

import jax
import jax.numpy as jnp
from jax import lax
from jax.experimental import pallas as pl
from jax.experimental.pallas import tpu as pltpu
from jax.sharding import PartitionSpec as P

F32 = jnp.float32
BF16 = jnp.bfloat16
UNROLL = 8
SMALL = 4 * 1024 * 1024


def in_hbm(*arrays):
    return [pltpu.with_memory_space_constraint(a, pltpu.HBM) for a in arrays]


def dot(a, b, dims):
    return lax.dot_general(a, b, (dims, ((), ())), preferred_element_type=F32)


def rating_kernel(
    user_idx_hbm, item_idx_hbm, target_hbm, count, users, items, ratings, grad_ref, mine_ref, hit_ref,
    user_idx, item_idx, target, items_t, pred, err, sem_s,
):
    n_tiles, tile = ratings.shape[0], ratings.shape[1]
    n_item = items.shape[0] // tile
    scalars = [
        pltpu.make_async_copy(source, target, sem_s.at[n])
        for n, (source, target) in enumerate(((target_hbm, target), (user_idx_hbm, user_idx), (item_idx_hbm, item_idx)))
    ]
    for copy in scalars:
        copy.start()
    own = mine_ref.shape[0]
    mine_ref[...] = items[pl.ds(pl.multiple_of(lax.axis_index("rows") * own, own), own), :]
    for j in range(n_item):
        items_t[j] = items[j * tile:(j + 1) * tile, :].T
    for first in range(0, n_item, 2):
        both = range(first, min(first + 2, n_item))
        whole = dot(users[...], jnp.concatenate([items_t[j] for j in both], axis=1), ((1,), (0,)))
        for n, j in enumerate(both):
            pred[j] = whole[:, n * tile:(n + 1) * tile]

    @pl.loop(0, users.shape[0] // tile)
    def _(c):
        for j in range(n_item):
            err[j, pl.ds(pl.multiple_of(c * tile, tile), tile), :] = jnp.zeros((tile, tile), F32)

    for copy in scalars:
        copy.wait()
    live = count[0, 0]
    for k in range(hit_ref.shape[0]):
        for j in range(n_item):
            hit_ref[k, j] = jnp.full((8, 128), (target[k] == j).astype(F32))

    def add_tile(t):
        j = item_idx[t]
        rows = pl.ds(pl.multiple_of(user_idx[t] * tile, tile), tile)
        diff = pred[j, rows, :] - ratings[t].astype(F32)
        err[j, rows, :] += diff.astype(BF16).astype(F32)

    groups = lax.div(live, UNROLL)

    @pl.loop(0, groups)
    def _(g):
        for k in range(UNROLL):
            add_tile(g * UNROLL + k)

    @pl.loop(groups * UNROLL, live)
    def _(t):
        add_tile(t)

    for j in range(n_item):
        whole = err[j]
        high = whole.astype(BF16)
        low = (whole - high.astype(F32)).astype(BF16)
        grad_ref[j * tile:(j + 1) * tile, :] = dot(high, users[...], ((0,), (0,))) + dot(low, users[...], ((0,), (0,)))


def rating_part(user_idx, item_idx, count, target, users, items, ratings, own_rows):
    tile = ratings.shape[1]
    n_item = items.shape[0] // tile
    smem = pl.BlockSpec(memory_space=pltpu.SMEM)
    hbm = pl.BlockSpec(memory_space=pltpu.HBM)
    vmem = pl.BlockSpec(memory_space=pltpu.VMEM)
    sums = pltpu.VMEM((n_item, users.shape[0], tile), F32)
    limit = 16 if n_item <= 2 else 56
    return pl.pallas_call(
        rating_kernel,
        name="rating_part",
        out_shape=(
            jax.ShapeDtypeStruct(items.shape, F32),
            jax.ShapeDtypeStruct((own_rows, items.shape[1]), BF16),
            jax.ShapeDtypeStruct((target.shape[0], n_item, 8, 128), F32),
        ),
        in_specs=[hbm] * 3 + [smem] + [vmem] * 3,
        out_specs=(vmem, vmem, vmem),
        scratch_shapes=[
            pltpu.SMEM(user_idx.shape, jnp.int32),
            pltpu.SMEM(item_idx.shape, jnp.int32),
            pltpu.SMEM(target.shape, jnp.int32),
            pltpu.VMEM((n_item, items.shape[1], tile), BF16),
            sums,
            sums,
            pltpu.SemaphoreType.DMA((3,)),
        ],
        compiler_params=pltpu.CompilerParams(vmem_limit_bytes=limit * 1024 * 1024),
    )(*in_hbm(user_idx, item_idx, target), count, users, items, ratings)


def pick_kernel(send_list_hbm, items_hbm, kept, sent, send_list, items, sem_s, sems):
    tile = kept.shape[0]
    copy_list = pltpu.make_async_copy(send_list_hbm, send_list, sem_s)
    copies = []
    for n in range(sems.shape[0]):
        rows = pl.ds(n * tile // 2, tile // 2)
        copies.append(pltpu.make_async_copy(items_hbm.at[rows], items.at[rows], sems.at[n]))
    for copy in copies:
        copy.start()
    copy_list.start()
    copy_list.wait()
    for copy in copies:
        copy.wait()
    me = lax.axis_index("cols")
    for out, col in ((kept, me), (sent, 1 - me)):
        out[...] = items[pl.ds(pl.multiple_of(send_list[col] * tile, tile), tile), :]


def pick_panels(send_list, items, tile):
    panel = jax.ShapeDtypeStruct((tile, items.shape[1]), BF16)
    vmem = pl.BlockSpec(memory_space=pltpu.VMEM)
    return pl.pallas_call(
        pick_kernel,
        name="pick_panels",
        out_shape=(panel, panel),
        in_specs=[pl.BlockSpec(memory_space=pltpu.HBM)] * 2,
        out_specs=(vmem, vmem),
        scratch_shapes=[
            pltpu.SMEM(send_list.shape, jnp.int32),
            pltpu.VMEM(items.shape, BF16),
            pltpu.SemaphoreType.DMA,
            pltpu.SemaphoreType.DMA((2 * items.shape[0] // tile,)),
        ],
        compiler_params=pltpu.CompilerParams(vmem_limit_bytes=SMALL),
        cost_estimate=pl.CostEstimate(flops=10**10, bytes_accessed=3 * 10**7, transcendentals=0),
    )(*in_hbm(send_list, items))


def parity(value):
    return bin(value).count("1") % 2


def hops(n_rows, odd):
    bits = [1 << b for b in range(1, n_rows.bit_length() - 1)]
    return bits[1:] + bits[:1] if odd else bits


def offset(n_rows, odd, q):
    value = sum(bit for b, bit in enumerate(hops(n_rows, odd)) if q >> b & 1)
    return value | parity(value)


def graph_kernel(n_panels, hit, grad, similarity, *refs):
    panels, outs, total = refs[:n_panels], refs[n_panels:-1], refs[-1]
    blocks, tile, unused = similarity.shape
    total[...] = grad[...]
    col = lax.axis_index("cols")
    for k in range(blocks):
        block = k if n_panels == 1 else k ^ col
        panel = panels[0][k] if n_panels == 1 else panels[k][...]
        part = dot(similarity[block], panel, ((1,), (0,)))
        for j in range(total.shape[0] // tile):
            chosen = jnp.broadcast_to(hit[block, j][:1, :1], part.shape) > 0
            total[j * tile:(j + 1) * tile, :] += jnp.where(chosen, part, 0)
    me = lax.axis_index("rows")
    if len(outs) == 1:
        outs[0][...] = total[...]
        return
    keep, give = outs
    half, own = keep.shape[:2]
    odd = sum((me >> b) & 1 for b in range(half.bit_length())) % 2
    for q in range(half):
        even_place, odd_place = (offset(2 * half, parity_, q) for parity_ in (0, 1))
        for out, block in (
            (keep, me ^ jnp.where(odd == 1, odd_place, even_place)),
            (give, me ^ 1 ^ jnp.where(odd == 1, even_place, odd_place)),
        ):
            out[q] = total[pl.ds(pl.multiple_of(block * own, own), own), :]


def graph_part(hit, grad, similarity, panels, out_shape):
    vmem = pl.BlockSpec(memory_space=pltpu.VMEM)
    return pl.pallas_call(
        functools.partial(graph_kernel, len(panels)),
        name="graph_part",
        out_shape=out_shape,
        in_specs=[vmem] * (3 + len(panels)),
        out_specs=jax.tree.map(lambda unused: vmem, out_shape),
        scratch_shapes=[pltpu.VMEM(grad.shape, F32)],
        compiler_params=pltpu.CompilerParams(vmem_limit_bytes=SMALL if grad.size <= 2**16 else 32 * 1024 * 1024),
    )(hit, grad, similarity, *panels)


def split_places(half, bit):
    return [q for q in range(half) if q & bit and not q & (bit - 1)]


def pack(total, payload, bit):
    half = total.shape[0]
    for q in range(half):
        payload[q] = total[q].astype(BF16)
    for n, q in enumerate(split_places(half, bit)):
        whole = total[q]
        payload[half + n] = (whole - whole.astype(BF16).astype(F32)).astype(BF16)


def unpack(received, q, bit, half):
    other = q ^ bit
    value = received[other].astype(F32)
    places = split_places(half, bit)
    if other in places:
        value = value + received[half + places.index(other)].astype(F32)
    return value


def first_kernel(keep, received, total, payload):
    total[...] = keep[...] + received[...]
    pack(total, payload, 1)


def next_kernel(bit, before, received, total, payload):
    half = total.shape[0]
    for q in range(half):
        total[q] = before[q] + unpack(received, q, bit, half)
    pack(total, payload, 2 * bit)


def last_kernel(bit, before, received, own, squares):
    half, rows, rank = before.shape
    part = jnp.zeros((8, 128), F32)
    for q in range(half):
        value = before[q] + unpack(received, q, bit, half)
        if q == 0:
            own[...] = value
        square = value * value
        for a in range(0, rows, 8):
            for b in range(0, rank, 128):
                part = part + square[a:a + 8, b:b + 128]
    squares[...] = part


def local_call(kernel, name, args, out_shape):
    vmem = pl.BlockSpec(memory_space=pltpu.VMEM)
    return pl.pallas_call(
        kernel, name=name, out_shape=out_shape, in_specs=[vmem] * len(args),
        out_specs=jax.tree.map(lambda unused: vmem, out_shape),
        compiler_params=pltpu.CompilerParams(vmem_limit_bytes=SMALL),
    )(*args)


def update_kernel(entries, mine, own, squares, more, new):
    meansq = jnp.sum(squares[...] + more[...], keepdims=True) / entries
    new[...] = mine[...].astype(F32) - 0.5 * own[...] / jnp.sqrt(meansq + 1e-06)


def swap(value, axis, bit):
    size = lax.axis_size(axis)
    return lax.ppermute(value, axis, [(i, i ^ bit) for i in range(size)])


def hop(value, b):
    size = lax.axis_size("rows")
    return lax.ppermute(value, "rows", [(i, i ^ 1 ^ hops(size, parity(i))[b]) for i in range(size)])


def shards(
    users, items, ratings, tile_users, tile_items, tile_count, send_list, block_target, similarity
):
    n_rows, n_cols = lax.axis_size("rows"), lax.axis_size("cols")
    icount, rank = items.shape[1:]
    tile = ratings.shape[-1]
    blocks = similarity.shape[2]
    panels = items[0].reshape(-1, tile, rank)
    slots = send_list.shape[3]
    if n_cols == 2 and slots == 1:
        kept, sent = pick_panels(send_list.reshape(-1), items[0], tile)
        incoming = (kept, swap(sent, "cols", 1))
    else:
        incoming = lax.all_to_all(panels[send_list[0, 0]], "cols", 0, 0, tiled=True)
        incoming = (incoming.reshape(blocks, tile, rank),)
    own_rows = icount // n_rows
    target = block_target.reshape(-1)
    grad, mine, hit = rating_part(
        tile_users.reshape(-1), tile_items.reshape(-1), tile_count, target, users, items[0],
        ratings[0, 0], own_rows,
    )
    entries = n_cols * icount * rank
    if n_rows & (n_rows - 1) or n_rows < 4 or n_cols != 2 or own_rows % 16:
        flat = graph_part(hit, grad, similarity[0, 0], incoming, (jax.ShapeDtypeStruct((icount, rank), F32),))[0]
        owned = lax.psum_scatter(flat, "rows", scatter_dimension=0, tiled=True)
        squares = lax.psum(jnp.sum(owned * owned), ("rows", "cols"))
        return (mine.astype(F32) - 0.5 * owned / jnp.sqrt(squares / entries + 1e-06))[None]

    half = n_rows // 2
    block = jax.ShapeDtypeStruct((half, own_rows, rank), F32)

    def payload(bit):
        return jax.ShapeDtypeStruct((half + len(split_places(half, bit)), own_rows, rank), BF16)

    keep, give = graph_part(hit, grad, similarity[0, 0], incoming, (block, block))
    total, sent = local_call(first_kernel, "add_core", (keep, swap(give, "rows", 1)), (block, payload(1)))
    n_hops = len(hops(n_rows, 0))
    for b in range(n_hops - 1):
        total, sent = local_call(
            functools.partial(next_kernel, 1 << b), "add_" + str(b), (total, hop(sent, b)), (block, payload(2 << b))
        )
    own, squares = local_call(
        functools.partial(last_kernel, half // 2), "add_last", (total, hop(sent, n_hops - 1)),
        (jax.ShapeDtypeStruct((own_rows, rank), F32), jax.ShapeDtypeStruct((8, 128), F32)),
    )
    squares = squares + swap(squares, "rows", 1)
    updated = local_call(
        functools.partial(update_kernel, entries), "update", (mine, own, squares, swap(squares, ("rows", "cols"), 3)),
        jax.ShapeDtypeStruct((own_rows, rank), F32),
    )
    return updated[None]


def solution(mesh):
    in_specs = (
        P("rows", None),
        P("cols", None, None),
        P("rows", "cols", None, None, None),
        P("rows", "cols", None),
        P("rows", "cols", None),
        P("rows", "cols"),
        P("rows", "cols", None, None),
        P("rows", "cols", None),
        P("rows", "cols", None, None, None),
    )
    out_specs = P("cols", "rows", None)
    return jax.shard_map(shards, mesh=mesh, in_specs=in_specs, out_specs=out_specs, check_vma=False)
```

```python
import functools

import jax
import jax.numpy as jnp
from jax import lax
from jax.experimental import pallas as pl
from jax.experimental.pallas import tpu as pltpu
from jax.sharding import PartitionSpec as P

F32 = jnp.float32
BF16 = jnp.bfloat16
UNROLL = 8
SMALL = 4 * 1024 * 1024


def in_hbm(*arrays):
    return [pltpu.with_memory_space_constraint(a, pltpu.HBM) for a in arrays]


def dot(a, b, dims):
    return lax.dot_general(a, b, (dims, ((), ())), preferred_element_type=F32)


def rating_kernel(
    user_idx_hbm, item_idx_hbm, target_hbm, count, users, items, ratings, grad_ref, mine_ref, hit_ref,
    user_idx, item_idx, target, items_t, pred, err, sem_s,
):
    n_tiles, tile = ratings.shape[0], ratings.shape[1]
    n_item = items.shape[0] // tile
    scalars = [
        pltpu.make_async_copy(source, target, sem_s.at[n])
        for n, (source, target) in enumerate(((target_hbm, target), (user_idx_hbm, user_idx), (item_idx_hbm, item_idx)))
    ]
    for copy in scalars:
        copy.start()
    own = mine_ref.shape[0]
    mine_ref[...] = items[pl.ds(pl.multiple_of(lax.axis_index("rows") * own, own), own), :]
    for j in range(n_item):
        items_t[j] = items[j * tile:(j + 1) * tile, :].T
    for first in range(0, n_item, 2):
        both = range(first, min(first + 2, n_item))
        whole = dot(users[...], jnp.concatenate([items_t[j] for j in both], axis=1), ((1,), (0,)))
        for n, j in enumerate(both):
            pred[j] = whole[:, n * tile:(n + 1) * tile]

    @pl.loop(0, users.shape[0] // tile)
    def _(c):
        for j in range(n_item):
            err[j, pl.ds(pl.multiple_of(c * tile, tile), tile), :] = jnp.zeros((tile, tile), F32)

    for copy in scalars:
        copy.wait()
    live = count[0, 0]
    for k in range(hit_ref.shape[0]):
        for j in range(n_item):
            hit_ref[k, j] = jnp.full((8, 128), (target[k] == j).astype(F32))

    def add_tile(t):
        j = item_idx[t]
        rows = pl.ds(pl.multiple_of(user_idx[t] * tile, tile), tile)
        diff = pred[j, rows, :] - ratings[t].astype(F32)
        err[j, rows, :] += diff.astype(BF16).astype(F32)

    groups = lax.div(live, UNROLL)

    @pl.loop(0, groups)
    def _(g):
        for k in range(UNROLL):
            add_tile(g * UNROLL + k)

    @pl.loop(groups * UNROLL, live)
    def _(t):
        add_tile(t)

    for j in range(n_item):
        whole = err[j]
        high = whole.astype(BF16)
        low = (whole - high.astype(F32)).astype(BF16)
        grad_ref[j * tile:(j + 1) * tile, :] = dot(high, users[...], ((0,), (0,))) + dot(low, users[...], ((0,), (0,)))


def rating_part(user_idx, item_idx, count, target, users, items, ratings, own_rows):
    tile = ratings.shape[1]
    n_item = items.shape[0] // tile
    smem = pl.BlockSpec(memory_space=pltpu.SMEM)
    hbm = pl.BlockSpec(memory_space=pltpu.HBM)
    vmem = pl.BlockSpec(memory_space=pltpu.VMEM)
    sums = pltpu.VMEM((n_item, users.shape[0], tile), F32)
    limit = 16 if n_item <= 2 else 56
    return pl.pallas_call(
        rating_kernel,
        name="rating_part",
        out_shape=(
            jax.ShapeDtypeStruct(items.shape, F32),
            jax.ShapeDtypeStruct((own_rows, items.shape[1]), BF16),
            jax.ShapeDtypeStruct((target.shape[0], n_item, 8, 128), F32),
        ),
        in_specs=[hbm] * 3 + [smem] + [vmem] * 3,
        out_specs=(vmem, vmem, vmem),
        scratch_shapes=[
            pltpu.SMEM(user_idx.shape, jnp.int32),
            pltpu.SMEM(item_idx.shape, jnp.int32),
            pltpu.SMEM(target.shape, jnp.int32),
            pltpu.VMEM((n_item, items.shape[1], tile), BF16),
            sums,
            sums,
            pltpu.SemaphoreType.DMA((3,)),
        ],
        compiler_params=pltpu.CompilerParams(vmem_limit_bytes=limit * 1024 * 1024),
    )(*in_hbm(user_idx, item_idx, target), count, users, items, ratings)


def pick_kernel(send_list_hbm, items_hbm, kept, sent, send_list, items, sem_s, sems):
    tile = kept.shape[0]
    copy_list = pltpu.make_async_copy(send_list_hbm, send_list, sem_s)
    copies = []
    for n in range(sems.shape[0]):
        rows = pl.ds(n * tile // 2, tile // 2)
        copies.append(pltpu.make_async_copy(items_hbm.at[rows], items.at[rows], sems.at[n]))
    for copy in copies:
        copy.start()
    copy_list.start()
    copy_list.wait()
    for copy in copies:
        copy.wait()
    me = lax.axis_index("cols")
    for out, col in ((kept, me), (sent, 1 - me)):
        out[...] = items[pl.ds(pl.multiple_of(send_list[col] * tile, tile), tile), :]


def pick_panels(send_list, items, tile):
    panel = jax.ShapeDtypeStruct((tile, items.shape[1]), BF16)
    vmem = pl.BlockSpec(memory_space=pltpu.VMEM)
    return pl.pallas_call(
        pick_kernel,
        name="pick_panels",
        out_shape=(panel, panel),
        in_specs=[pl.BlockSpec(memory_space=pltpu.HBM)] * 2,
        out_specs=(vmem, vmem),
        scratch_shapes=[
            pltpu.SMEM(send_list.shape, jnp.int32),
            pltpu.VMEM(items.shape, BF16),
            pltpu.SemaphoreType.DMA,
            pltpu.SemaphoreType.DMA((2 * items.shape[0] // tile,)),
        ],
        compiler_params=pltpu.CompilerParams(vmem_limit_bytes=SMALL),
        cost_estimate=pl.CostEstimate(flops=10**10, bytes_accessed=3 * 10**7, transcendentals=0),
    )(*in_hbm(send_list, items))


def parity(value):
    return bin(value).count("1") % 2


def hops(n_rows, odd):
    bits = [1 << b for b in range(1, n_rows.bit_length() - 1)]
    return bits[1:] + bits[:1] if odd else bits


def offset(n_rows, odd, q):
    value = sum(bit for b, bit in enumerate(hops(n_rows, odd)) if q >> b & 1)
    return value | parity(value)


def graph_kernel(n_panels, hit, grad, similarity, *refs):
    panels, outs, total = refs[:n_panels], refs[n_panels:-1], refs[-1]
    blocks, tile, unused = similarity.shape
    col = lax.axis_index("cols")
    parts = []
    for k in range(blocks):
        block = k if n_panels == 1 else k ^ col
        panel = panels[0][k] if n_panels == 1 else panels[k][...]
        parts.append((block, dot(similarity[block], panel, ((1,), (0,)))))
    for j in range(total.shape[0] // tile):
        value = grad[j * tile:(j + 1) * tile, :]
        for block, part in parts:
            value += jnp.where(jnp.broadcast_to(hit[block, j][:1, :1], part.shape) > 0, part, 0)
        total[j * tile:(j + 1) * tile, :] = value
    me = lax.axis_index("rows")
    if len(outs) == 1:
        outs[0][...] = total[...]
        return
    keep, give = outs
    half, own = keep.shape[:2]
    odd = sum((me >> b) & 1 for b in range(half.bit_length())) % 2
    for q in range(half):
        even_place, odd_place = (offset(2 * half, parity_, q) for parity_ in (0, 1))
        for out, block in (
            (keep, me ^ jnp.where(odd == 1, odd_place, even_place)),
            (give, me ^ 1 ^ jnp.where(odd == 1, even_place, odd_place)),
        ):
            out[q] = total[pl.ds(pl.multiple_of(block * own, own), own), :]


def graph_part(hit, grad, similarity, panels, out_shape):
    vmem = pl.BlockSpec(memory_space=pltpu.VMEM)
    return pl.pallas_call(
        functools.partial(graph_kernel, len(panels)),
        name="graph_part",
        out_shape=out_shape,
        in_specs=[vmem] * (3 + len(panels)),
        out_specs=jax.tree.map(lambda unused: vmem, out_shape),
        scratch_shapes=[pltpu.VMEM(grad.shape, F32)],
        compiler_params=pltpu.CompilerParams(vmem_limit_bytes=SMALL if grad.size <= 2**16 else 32 * 1024 * 1024),
    )(hit, grad, similarity, *panels)


def split_places(half, bit):
    return [q for q in range(half) if q & bit and not q & (bit - 1)]


def pack(total, payload, bit):
    half = total.shape[0]
    for q in range(half):
        payload[q] = total[q].astype(BF16)
    for n, q in enumerate(split_places(half, bit)):
        whole = total[q]
        payload[half + n] = (whole - whole.astype(BF16).astype(F32)).astype(BF16)


def unpack(received, q, bit, half):
    other = q ^ bit
    value = received[other].astype(F32)
    places = split_places(half, bit)
    if other in places:
        value = value + received[half + places.index(other)].astype(F32)
    return value


def first_kernel(keep, received, total, payload):
    total[...] = keep[...] + received[...]
    pack(total, payload, 1)


def next_kernel(bit, before, received, total, payload):
    half = total.shape[0]
    for q in range(half):
        total[q] = before[q] + unpack(received, q, bit, half)
    pack(total, payload, 2 * bit)


def last_kernel(bit, before, received, own, squares):
    half, rows, rank = before.shape
    part = jnp.zeros((8, 128), F32)
    for q in range(half):
        value = before[q] + unpack(received, q, bit, half)
        if q == 0:
            own[...] = value
        square = value * value
        for a in range(0, rows, 8):
            for b in range(0, rank, 128):
                part = part + square[a:a + 8, b:b + 128]
    squares[...] = jnp.sum(part, axis=0, keepdims=True)


def local_call(kernel, name, args, out_shape):
    vmem = pl.BlockSpec(memory_space=pltpu.VMEM)
    return pl.pallas_call(
        kernel, name=name, out_shape=out_shape, in_specs=[vmem] * len(args),
        out_specs=jax.tree.map(lambda unused: vmem, out_shape),
        compiler_params=pltpu.CompilerParams(vmem_limit_bytes=SMALL),
    )(*args)


def update_kernel(entries, mine, own, squares, more, new):
    meansq = jnp.sum(jnp.broadcast_to(squares[...] + more[...], (8, 128)), axis=1, keepdims=True)[:1] * (1 / entries)
    new[...] = mine[...].astype(F32) - own[...] * (0.5 * lax.rsqrt(meansq + 1e-06))


def swap(value, axis, bit):
    size = lax.axis_size(axis)
    return lax.ppermute(value, axis, [(i, i ^ bit) for i in range(size)])


def hop(value, b):
    size = lax.axis_size("rows")
    return lax.ppermute(value, "rows", [(i, i ^ 1 ^ hops(size, parity(i))[b]) for i in range(size)])


def shards(
    users, items, ratings, tile_users, tile_items, tile_count, send_list, block_target, similarity
):
    n_rows, n_cols = lax.axis_size("rows"), lax.axis_size("cols")
    icount, rank = items.shape[1:]
    tile = ratings.shape[-1]
    blocks = similarity.shape[2]
    panels = items[0].reshape(-1, tile, rank)
    slots = send_list.shape[3]
    if n_cols == 2 and slots == 1:
        kept, sent = pick_panels(send_list.reshape(-1), items[0], tile)
        incoming = (kept, swap(sent, "cols", 1))
    else:
        incoming = lax.all_to_all(panels[send_list[0, 0]], "cols", 0, 0, tiled=True)
        incoming = (incoming.reshape(blocks, tile, rank),)
    own_rows = icount // n_rows
    target = block_target.reshape(-1)
    grad, mine, hit = rating_part(
        tile_users.reshape(-1), tile_items.reshape(-1), tile_count, target, users, items[0],
        ratings[0, 0], own_rows,
    )
    entries = n_cols * icount * rank
    if n_rows & (n_rows - 1) or n_rows < 4 or n_cols != 2 or own_rows % 16:
        flat = graph_part(hit, grad, similarity[0, 0], incoming, (jax.ShapeDtypeStruct((icount, rank), F32),))[0]
        owned = lax.psum_scatter(flat, "rows", scatter_dimension=0, tiled=True)
        squares = lax.psum(jnp.sum(owned * owned), ("rows", "cols"))
        return (mine.astype(F32) - 0.5 * owned / jnp.sqrt(squares / entries + 1e-06))[None]

    half = n_rows // 2
    block = jax.ShapeDtypeStruct((half, own_rows, rank), F32)

    def payload(bit):
        return jax.ShapeDtypeStruct((half + len(split_places(half, bit)), own_rows, rank), BF16)

    keep, give = graph_part(hit, grad, similarity[0, 0], incoming, (block, block))
    total, sent = local_call(first_kernel, "add_core", (keep, swap(give, "rows", 1)), (block, payload(1)))
    n_hops = len(hops(n_rows, 0))
    for b in range(n_hops - 1):
        total, sent = local_call(
            functools.partial(next_kernel, 1 << b), "add_" + str(b), (total, hop(sent, b)), (block, payload(2 << b))
        )
    own, squares = local_call(
        functools.partial(last_kernel, half // 2), "add_last", (total, hop(sent, n_hops - 1)),
        (jax.ShapeDtypeStruct((own_rows, rank), F32), jax.ShapeDtypeStruct((1, 128), F32)),
    )
    squares = squares + swap(squares, "rows", 1)
    updated = local_call(
        functools.partial(update_kernel, entries), "update", (mine, own, squares, swap(squares, ("rows", "cols"), 3)),
        jax.ShapeDtypeStruct((own_rows, rank), F32),
    )
    return updated[None]


def solution(mesh):
    in_specs = (
        P("rows", None),
        P("cols", None, None),
        P("rows", "cols", None, None, None),
        P("rows", "cols", None),
        P("rows", "cols", None),
        P("rows", "cols"),
        P("rows", "cols", None, None),
        P("rows", "cols", None),
        P("rows", "cols", None, None, None),
    )
    out_specs = P("cols", "rows", None)
    return jax.shard_map(shards, mesh=mesh, in_specs=in_specs, out_specs=out_specs, check_vma=False)
```

```python
import functools

import jax
import jax.numpy as jnp
from jax import lax
from jax.experimental import pallas as pl
from jax.experimental.pallas import tpu as pltpu
from jax.sharding import PartitionSpec as P

F32 = jnp.float32
BF16 = jnp.bfloat16
UNROLL = 8
SMALL = 4 * 1024 * 1024


def in_hbm(*arrays):
    return [pltpu.with_memory_space_constraint(a, pltpu.HBM) for a in arrays]


def dot(a, b, dims):
    return lax.dot_general(a, b, (dims, ((), ())), preferred_element_type=F32)


def rating_kernel(half, user_idx_hbm, item_idx_hbm, target_hbm, count, users, items, ratings, similarity, near, *refs):
    grad_out, mine_ref, keep_far, give_far, give_out = refs[:5]
    grad_ref, far_ref, user_idx, item_idx, target, items_t, pred, err, sem_s = refs[5:]
    n_tiles, tile = ratings.shape[0], ratings.shape[1]
    n_item = items.shape[0] // tile
    scalars = [
        pltpu.make_async_copy(source, target, sem_s.at[n])
        for n, (source, target) in enumerate(((target_hbm, target), (user_idx_hbm, user_idx), (item_idx_hbm, item_idx)))
    ]
    for copy in scalars:
        copy.start()
    own = mine_ref.shape[0]
    mine_ref[...] = items[pl.ds(pl.multiple_of(lax.axis_index("rows") * own, own), own), :]
    for j in range(n_item):
        items_t[j] = items[j * tile:(j + 1) * tile, :].T
    for first in range(0, n_item, 2):
        both = range(first, min(first + 2, n_item))
        whole = dot(users[...], jnp.concatenate([items_t[j] for j in both], axis=1), ((1,), (0,)))
        for n, j in enumerate(both):
            pred[j] = whole[:, n * tile:(n + 1) * tile]

    @pl.loop(0, users.shape[0] // tile)
    def _(c):
        for j in range(n_item):
            err[j, pl.ds(pl.multiple_of(c * tile, tile), tile), :] = jnp.zeros((tile, tile), F32)

    for copy in scalars:
        copy.wait()
    live = count[0, 0]
    col = lax.axis_index("cols")
    block = similarity[1 - col]
    for j in range(n_item):
        far_ref[j * tile:(j + 1) * tile, :] = jnp.where(target[1 - col] == j, block, jnp.zeros_like(block))

    def add_tile(t):
        j = item_idx[t]
        rows = pl.ds(pl.multiple_of(user_idx[t] * tile, tile), tile)
        diff = pred[j, rows, :] - ratings[t].astype(F32)
        err[j, rows, :] += diff.astype(BF16).astype(F32)

    groups = lax.div(live, UNROLL)

    @pl.loop(0, groups)
    def _(g):
        for k in range(UNROLL):
            add_tile(g * UNROLL + k)

    @pl.loop(groups * UNROLL, live)
    def _(t):
        add_tile(t)

    for j in range(n_item):
        whole = err[j]
        high = whole.astype(BF16)
        low = (whole - high.astype(F32)).astype(BF16)
        whole = dot(jnp.concatenate([high, low], axis=1), users[...], ((0,), (0,)))
        grad_ref[j * tile:(j + 1) * tile, :] = whole[:tile] + whole[tile:]
    if not half:
        grad_out[...] = grad_ref[...]
        return
    rows = pl.ds(pl.multiple_of(target[col] * tile, tile), tile)
    grad_ref[rows, :] += dot(similarity[col], near[...], ((1,), (0,)))
    me = lax.axis_index("rows")
    odd = sum((me >> b) & 1 for b in range(half.bit_length())) % 2
    for q in range(half):
        even_place, odd_place = (offset(2 * half, parity_, q) for parity_ in (0, 1))
        span = slice(q * own, (q + 1) * own)
        for out, far_out, place in (
            (grad_out, keep_far, me ^ jnp.where(odd == 1, odd_place, even_place)),
            (give_out, give_far, me ^ 1 ^ jnp.where(odd == 1, even_place, odd_place)),
        ):
            rows = pl.ds(pl.multiple_of(place * own, own), own)
            out[span, :] = grad_ref[rows, :]
            far_out[span, :] = far_ref[rows, :]


def rating_part(user_idx, item_idx, count, target, users, items, ratings, similarity, near, own_rows, half):
    tile = ratings.shape[1]
    n_item = items.shape[0] // tile
    smem = pl.BlockSpec(memory_space=pltpu.SMEM)
    hbm = pl.BlockSpec(memory_space=pltpu.HBM)
    vmem = pl.BlockSpec(memory_space=pltpu.VMEM)
    sums = pltpu.VMEM((n_item, users.shape[0], tile), F32)
    limit = 16 if n_item <= 2 else 56
    count_rows = half * own_rows if half else items.shape[0]
    rows = jax.ShapeDtypeStruct((count_rows, items.shape[1]), F32)
    far_rows = jax.ShapeDtypeStruct((count_rows, tile), BF16)
    return pl.pallas_call(
        functools.partial(rating_kernel, half),
        name="rating_part",
        out_shape=(rows, jax.ShapeDtypeStruct((own_rows, items.shape[1]), BF16), far_rows, far_rows, rows),
        in_specs=[hbm] * 3 + [smem] + [vmem] * 5,
        out_specs=(vmem,) * 5,
        scratch_shapes=[
            pltpu.VMEM(items.shape, F32),
            pltpu.VMEM((items.shape[0], tile), BF16),
            pltpu.SMEM(user_idx.shape, jnp.int32),
            pltpu.SMEM(item_idx.shape, jnp.int32),
            pltpu.SMEM(target.shape, jnp.int32),
            pltpu.VMEM((n_item, items.shape[1], tile), BF16),
            sums,
            sums,
            pltpu.SemaphoreType.DMA((3,)),
        ],
        compiler_params=pltpu.CompilerParams(vmem_limit_bytes=limit * 1024 * 1024),
    )(*in_hbm(user_idx, item_idx, target), count, users, items, ratings, similarity, near)


def pick_kernel(send_list_hbm, items_hbm, kept, sent, send_list, items, sem_s, sems):
    tile = kept.shape[0]
    copy_list = pltpu.make_async_copy(send_list_hbm, send_list, sem_s)
    copies = []
    for n in range(sems.shape[0]):
        rows = pl.ds(n * tile // 2, tile // 2)
        copies.append(pltpu.make_async_copy(items_hbm.at[rows], items.at[rows], sems.at[n]))
    for copy in copies:
        copy.start()
    copy_list.start()
    copy_list.wait()
    for copy in copies:
        copy.wait()
    me = lax.axis_index("cols")
    for out, col in ((kept, me), (sent, 1 - me)):
        out[...] = items[pl.ds(pl.multiple_of(send_list[col] * tile, tile), tile), :]


def pick_panels(send_list, items, tile):
    panel = jax.ShapeDtypeStruct((tile, items.shape[1]), BF16)
    vmem = pl.BlockSpec(memory_space=pltpu.VMEM)
    return pl.pallas_call(
        pick_kernel,
        name="pick_panels",
        out_shape=(panel, panel),
        in_specs=[pl.BlockSpec(memory_space=pltpu.HBM)] * 2,
        out_specs=(vmem, vmem),
        scratch_shapes=[
            pltpu.SMEM(send_list.shape, jnp.int32),
            pltpu.VMEM(items.shape, BF16),
            pltpu.SemaphoreType.DMA,
            pltpu.SemaphoreType.DMA((2 * items.shape[0] // tile,)),
        ],
        compiler_params=pltpu.CompilerParams(vmem_limit_bytes=SMALL),
        cost_estimate=pl.CostEstimate(flops=10**10, bytes_accessed=3 * 10**7, transcendentals=0),
    )(*in_hbm(send_list, items))


def parity(value):
    return bin(value).count("1") % 2


def hops(n_rows, odd):
    bits = [1 << b for b in range(1, n_rows.bit_length() - 1)]
    return bits[1:] + bits[:1] if odd else bits


def offset(n_rows, odd, q):
    value = sum(bit for b, bit in enumerate(hops(n_rows, odd)) if q >> b & 1)
    return value | parity(value)


def graph_kernel(grad, far_blocks, far, total):
    whole = grad[...] + dot(far_blocks[...], far[...], ((1,), (0,)))
    total[...] = whole.reshape(total.shape)


def split_places(half, bit):
    return [q for q in range(half) if q & bit and not q & (bit - 1)]


def pack(total, payload, bit):
    half = total.shape[0]
    for q in range(half):
        payload[q] = total[q].astype(BF16)
    for n, q in enumerate(split_places(half, bit)):
        whole = total[q]
        payload[half + n] = (whole - whole.astype(BF16).astype(F32)).astype(BF16)


def unpack(received, q, bit, half):
    other = q ^ bit
    value = received[other].astype(F32)
    places = split_places(half, bit)
    if other in places:
        value = value + received[half + places.index(other)].astype(F32)
    return value


def first_kernel(keep, received, total, payload):
    total[...] = keep[...] + received[...]
    pack(total, payload, 1)


def next_kernel(bit, before, received, total, payload):
    half = total.shape[0]
    for q in range(half):
        total[q] = before[q] + unpack(received, q, bit, half)
    pack(total, payload, 2 * bit)


def last_kernel(bit, before, received, own, squares):
    half, rows, rank = before.shape
    part = jnp.zeros((8, 128), F32)
    for q in range(half):
        value = before[q] + unpack(received, q, bit, half)
        if q == 0:
            own[...] = value
        square = value * value
        for a in range(0, rows, 8):
            for b in range(0, rank, 128):
                part = part + square[a:a + 8, b:b + 128]
    squares[...] = jnp.sum(part, axis=0, keepdims=True)


def local_call(kernel, name, args, out_shape):
    vmem = pl.BlockSpec(memory_space=pltpu.VMEM)
    return pl.pallas_call(
        kernel, name=name, out_shape=out_shape, in_specs=[vmem] * len(args),
        out_specs=jax.tree.map(lambda unused: vmem, out_shape),
        compiler_params=pltpu.CompilerParams(vmem_limit_bytes=SMALL),
    )(*args)


def update_kernel(entries, mine, own, squares, more, new):
    meansq = jnp.sum(jnp.broadcast_to(squares[...] + more[...], (8, 128)), axis=1, keepdims=True)[:1] * (1 / entries)
    new[...] = mine[...].astype(F32) - own[...] * (0.5 * lax.rsqrt(meansq + 1e-06))


def swap(value, axis, bit):
    size = lax.axis_size(axis)
    return lax.ppermute(value, axis, [(i, i ^ bit) for i in range(size)])


def hop(value, b):
    size = lax.axis_size("rows")
    return lax.ppermute(value, "rows", [(i, i ^ 1 ^ hops(size, parity(i))[b]) for i in range(size)])


def shards(
    users, items, ratings, tile_users, tile_items, tile_count, send_list, block_target, similarity
):
    n_rows, n_cols = lax.axis_size("rows"), lax.axis_size("cols")
    icount, rank = items.shape[1:]
    tile = ratings.shape[-1]
    blocks = similarity.shape[2]
    slots = send_list.shape[3]
    own_rows = icount // n_rows
    target = block_target.reshape(-1)
    entries = n_cols * icount * rank
    by_hops = n_rows >= 4 and not n_rows & (n_rows - 1) and n_cols == 2 and slots == 1 and own_rows % 16 == 0
    if by_hops:
        near, sent = pick_panels(send_list.reshape(-1), items[0], tile)
        far = swap(sent, "cols", 1)
    else:
        panels = items[0].reshape(-1, tile, rank)
        incoming = lax.all_to_all(panels[send_list[0, 0]], "cols", 0, 0, tiled=True)
        incoming = incoming.reshape(blocks, tile, rank)
        near = jnp.zeros((tile, rank), BF16)
    half = n_rows // 2 if by_hops else 0
    grad, mine, keep_far, give_far, given = rating_part(
        tile_users.reshape(-1), tile_items.reshape(-1), tile_count, target, users, items[0], ratings[0, 0],
        similarity[0, 0, :2], near, own_rows, half,
    )
    if not by_hops:
        contrib = jnp.einsum("kab,kbr->kar", similarity[0, 0], incoming, preferred_element_type=F32)
        flat = grad.reshape(-1, tile, rank).at[target].add(contrib).reshape(icount, rank)
        owned = lax.psum_scatter(flat, "rows", scatter_dimension=0, tiled=True)
        squares = lax.psum(jnp.sum(owned * owned), ("rows", "cols"))
        return (mine.astype(F32) - 0.5 * owned / jnp.sqrt(squares / entries + 1e-06))[None]

    block = jax.ShapeDtypeStruct((half, own_rows, rank), F32)

    def payload(bit):
        return jax.ShapeDtypeStruct((half + len(split_places(half, bit)), own_rows, rank), BF16)

    give = local_call(graph_kernel, "graph_give", (given, give_far, far), block)
    keep = local_call(graph_kernel, "graph_keep", (grad, keep_far, far), block)
    total, sent = local_call(first_kernel, "add_core", (keep, swap(give, "rows", 1)), (block, payload(1)))
    n_hops = len(hops(n_rows, 0))
    for b in range(n_hops - 1):
        total, sent = local_call(
            functools.partial(next_kernel, 1 << b), "add_" + str(b), (total, hop(sent, b)), (block, payload(2 << b))
        )
    own, squares = local_call(
        functools.partial(last_kernel, half // 2), "add_last", (total, hop(sent, n_hops - 1)),
        (jax.ShapeDtypeStruct((own_rows, rank), F32), jax.ShapeDtypeStruct((1, 128), F32)),
    )
    squares = squares + swap(squares, "rows", 1)
    updated = local_call(
        functools.partial(update_kernel, entries), "update", (mine, own, squares, swap(squares, ("rows", "cols"), 3)),
        jax.ShapeDtypeStruct((own_rows, rank), F32),
    )
    return updated[None]


def solution(mesh):
    in_specs = (
        P("rows", None),
        P("cols", None, None),
        P("rows", "cols", None, None, None),
        P("rows", "cols", None),
        P("rows", "cols", None),
        P("rows", "cols"),
        P("rows", "cols", None, None),
        P("rows", "cols", None),
        P("rows", "cols", None, None, None),
    )
    out_specs = P("cols", "rows", None)
    return jax.shard_map(shards, mesh=mesh, in_specs=in_specs, out_specs=out_specs, check_vma=False)
```

```python
import functools

import jax
import jax.numpy as jnp
from jax import lax
from jax.experimental import pallas as pl
from jax.experimental.pallas import tpu as pltpu
from jax.sharding import PartitionSpec as P

F32 = jnp.float32
BF16 = jnp.bfloat16
UNROLL = 8
SMALL = 4 * 1024 * 1024


def in_hbm(*arrays):
    return [pltpu.with_memory_space_constraint(a, pltpu.HBM) for a in arrays]


def dot(a, b, dims):
    return lax.dot_general(a, b, (dims, ((), ())), preferred_element_type=F32)


def rating_kernel(half, user_idx_hbm, item_idx_hbm, target_hbm, count, list_hbm, users, items, ratings, similarity, *refs):
    grad_out, mine_ref, keep_far, give_far, give_out = refs[:5]
    grad_ref, far_ref, user_idx, item_idx, target, send_list, items_t, pred, err, sem_s = refs[5:]
    n_tiles, tile = ratings.shape[0], ratings.shape[1]
    n_item = items.shape[0] // tile
    scalars = [
        pltpu.make_async_copy(source, place, sem_s.at[n])
        for n, (source, place) in enumerate(
            ((target_hbm, target), (list_hbm, send_list), (user_idx_hbm, user_idx), (item_idx_hbm, item_idx))
        )
    ]
    for copy in scalars:
        copy.start()
    own = mine_ref.shape[0]
    mine_ref[...] = items[pl.ds(pl.multiple_of(lax.axis_index("rows") * own, own), own), :]
    for j in range(n_item):
        items_t[j] = items[j * tile:(j + 1) * tile, :].T
    for first in range(0, n_item, 2):
        both = range(first, min(first + 2, n_item))
        whole = dot(users[...], jnp.concatenate([items_t[j] for j in both], axis=1), ((1,), (0,)))
        for n, j in enumerate(both):
            pred[j] = whole[:, n * tile:(n + 1) * tile]

    @pl.loop(0, users.shape[0] // tile)
    def _(c):
        for j in range(n_item):
            err[j, pl.ds(pl.multiple_of(c * tile, tile), tile), :] = jnp.zeros((tile, tile), F32)

    for copy in scalars:
        copy.wait()
    live = count[0, 0]
    col = lax.axis_index("cols")
    block = similarity[1 - col]
    for j in range(n_item):
        far_ref[j * tile:(j + 1) * tile, :] = jnp.where(target[1 - col] == j, block, jnp.zeros_like(block))

    def add_tile(t):
        j = item_idx[t]
        rows = pl.ds(pl.multiple_of(user_idx[t] * tile, tile), tile)
        diff = pred[j, rows, :] - ratings[t].astype(F32)
        err[j, rows, :] += diff.astype(BF16).astype(F32)

    groups = lax.div(live, UNROLL)

    @pl.loop(0, groups)
    def _(g):
        for k in range(UNROLL):
            add_tile(g * UNROLL + k)

    @pl.loop(groups * UNROLL, live)
    def _(t):
        add_tile(t)

    for j in range(n_item):
        whole = err[j]
        high = whole.astype(BF16)
        low = (whole - high.astype(F32)).astype(BF16)
        whole = dot(jnp.concatenate([high, low], axis=1), users[...], ((0,), (0,)))
        grad_ref[j * tile:(j + 1) * tile, :] = whole[:tile] + whole[tile:]
    if not half:
        grad_out[...] = grad_ref[...]
        return
    rows = pl.ds(pl.multiple_of(target[col] * tile, tile), tile)
    near = items[pl.ds(pl.multiple_of(send_list[col] * tile, tile), tile), :]
    grad_ref[rows, :] += dot(similarity[col], near, ((1,), (0,)))
    me = lax.axis_index("rows")
    odd = sum((me >> b) & 1 for b in range(half.bit_length())) % 2
    for q in range(half):
        even_place, odd_place = (offset(2 * half, parity_, q) for parity_ in (0, 1))
        span = slice(q * own, (q + 1) * own)
        for out, far_out, place in (
            (grad_out, keep_far, me ^ jnp.where(odd == 1, odd_place, even_place)),
            (give_out, give_far, me ^ 1 ^ jnp.where(odd == 1, even_place, odd_place)),
        ):
            rows = pl.ds(pl.multiple_of(place * own, own), own)
            out[span, :] = grad_ref[rows, :]
            far_out[span, :] = far_ref[rows, :]


def rating_part(user_idx, item_idx, count, target, send_list, users, items, ratings, similarity, own_rows, half):
    tile = ratings.shape[1]
    n_item = items.shape[0] // tile
    smem = pl.BlockSpec(memory_space=pltpu.SMEM)
    hbm = pl.BlockSpec(memory_space=pltpu.HBM)
    vmem = pl.BlockSpec(memory_space=pltpu.VMEM)
    sums = pltpu.VMEM((n_item, users.shape[0], tile), F32)
    limit = 16 if n_item <= 2 else 56
    count_rows = half * own_rows if half else items.shape[0]
    rows = jax.ShapeDtypeStruct((count_rows, items.shape[1]), F32)
    far_rows = jax.ShapeDtypeStruct((count_rows, tile), BF16)
    return pl.pallas_call(
        functools.partial(rating_kernel, half),
        name="rating_part",
        out_shape=(rows, jax.ShapeDtypeStruct((own_rows, items.shape[1]), BF16), far_rows, far_rows, rows),
        in_specs=[hbm] * 3 + [smem, hbm] + [vmem] * 4,
        out_specs=(vmem,) * 5,
        scratch_shapes=[
            pltpu.VMEM(items.shape, F32),
            pltpu.VMEM((items.shape[0], tile), BF16),
            pltpu.SMEM(user_idx.shape, jnp.int32),
            pltpu.SMEM(item_idx.shape, jnp.int32),
            pltpu.SMEM(target.shape, jnp.int32),
            pltpu.SMEM(send_list.shape, jnp.int32),
            pltpu.VMEM((n_item, items.shape[1], tile), BF16),
            sums,
            sums,
            pltpu.SemaphoreType.DMA((4,)),
        ],
        compiler_params=pltpu.CompilerParams(vmem_limit_bytes=limit * 1024 * 1024),
    )(*in_hbm(user_idx, item_idx, target), count, *in_hbm(send_list), users, items, ratings, similarity)


def pick_kernel(send_list_hbm, items_hbm, sent, send_list, items, sem_s, sems):
    tile = sent.shape[0]
    copy_list = pltpu.make_async_copy(send_list_hbm, send_list, sem_s)
    copies = []
    for n in range(sems.shape[0]):
        rows = pl.ds(n * tile // 2, tile // 2)
        copies.append(pltpu.make_async_copy(items_hbm.at[rows], items.at[rows], sems.at[n]))
    for copy in copies:
        copy.start()
    copy_list.start()
    copy_list.wait()
    for copy in copies:
        copy.wait()
    me = lax.axis_index("cols")
    sent[...] = items[pl.ds(pl.multiple_of(send_list[1 - me] * tile, tile), tile), :]


def pick_panels(send_list, items, tile):
    panel = jax.ShapeDtypeStruct((tile, items.shape[1]), BF16)
    vmem = pl.BlockSpec(memory_space=pltpu.VMEM)
    return pl.pallas_call(
        pick_kernel,
        name="pick_panels",
        out_shape=panel,
        in_specs=[pl.BlockSpec(memory_space=pltpu.HBM)] * 2,
        out_specs=vmem,
        scratch_shapes=[
            pltpu.SMEM(send_list.shape, jnp.int32),
            pltpu.VMEM(items.shape, BF16),
            pltpu.SemaphoreType.DMA,
            pltpu.SemaphoreType.DMA((2 * items.shape[0] // tile,)),
        ],
        compiler_params=pltpu.CompilerParams(vmem_limit_bytes=SMALL),
        cost_estimate=pl.CostEstimate(flops=10**10, bytes_accessed=3 * 10**7, transcendentals=0),
    )(*in_hbm(send_list, items))


def parity(value):
    return bin(value).count("1") % 2


def hops(n_rows, odd):
    bits = [1 << b for b in range(1, n_rows.bit_length() - 1)]
    return bits[1:] + bits[:1] if odd else bits


def offset(n_rows, odd, q):
    value = sum(bit for b, bit in enumerate(hops(n_rows, odd)) if q >> b & 1)
    return value | parity(value)


def graph_kernel(grad, far_blocks, far, total):
    whole = grad[...] + dot(far_blocks[...], far[...], ((1,), (0,)))
    total[...] = whole.reshape(total.shape)


def split_places(half, bit):
    return [q for q in range(half) if q & bit and not q & (bit - 1)]


def pack(total, payload, bit):
    half = total.shape[0]
    for q in range(half):
        payload[q] = total[q].astype(BF16)
    for n, q in enumerate(split_places(half, bit)):
        whole = total[q]
        payload[half + n] = (whole - whole.astype(BF16).astype(F32)).astype(BF16)


def unpack(received, q, bit, half):
    other = q ^ bit
    value = received[other].astype(F32)
    places = split_places(half, bit)
    if other in places:
        value = value + received[half + places.index(other)].astype(F32)
    return value


def first_kernel(keep, received, total, payload):
    total[...] = keep[...] + received[...]
    pack(total, payload, 1)


def next_kernel(bit, before, received, total, payload):
    half = total.shape[0]
    for q in range(half):
        total[q] = before[q] + unpack(received, q, bit, half)
    pack(total, payload, 2 * bit)


def last_kernel(bit, before, received, own, squares):
    half, rows, rank = before.shape
    part = jnp.zeros((8, 128), F32)
    for q in range(half):
        value = before[q] + unpack(received, q, bit, half)
        if q == 0:
            own[...] = value
        square = value * value
        for a in range(0, rows, 8):
            for b in range(0, rank, 128):
                part = part + square[a:a + 8, b:b + 128]
    squares[...] = jnp.sum(part, axis=0, keepdims=True)


def local_call(kernel, name, args, out_shape):
    vmem = pl.BlockSpec(memory_space=pltpu.VMEM)
    return pl.pallas_call(
        kernel, name=name, out_shape=out_shape, in_specs=[vmem] * len(args),
        out_specs=jax.tree.map(lambda unused: vmem, out_shape),
        compiler_params=pltpu.CompilerParams(vmem_limit_bytes=SMALL),
    )(*args)


def update_kernel(entries, mine, own, squares, more, new):
    meansq = jnp.sum(jnp.broadcast_to(squares[...] + more[...], (8, 128)), axis=1, keepdims=True)[:1] * (1 / entries)
    new[...] = mine[...].astype(F32) - own[...] * (0.5 * lax.rsqrt(meansq + 1e-06))


def swap(value, axis, bit):
    size = lax.axis_size(axis)
    return lax.ppermute(value, axis, [(i, i ^ bit) for i in range(size)])


def hop(value, b):
    size = lax.axis_size("rows")
    return lax.ppermute(value, "rows", [(i, i ^ 1 ^ hops(size, parity(i))[b]) for i in range(size)])


def shards(
    users, items, ratings, tile_users, tile_items, tile_count, send_list, block_target, similarity
):
    n_rows, n_cols = lax.axis_size("rows"), lax.axis_size("cols")
    icount, rank = items.shape[1:]
    tile = ratings.shape[-1]
    blocks = similarity.shape[2]
    slots = send_list.shape[3]
    own_rows = icount // n_rows
    target = block_target.reshape(-1)
    entries = n_cols * icount * rank
    by_hops = n_rows >= 4 and not n_rows & (n_rows - 1) and n_cols == 2 and slots == 1 and own_rows % 16 == 0
    if by_hops:
        sent = pick_panels(send_list.reshape(-1), items[0], tile)
        far = swap(sent, "cols", 1)
    else:
        panels = items[0].reshape(-1, tile, rank)
        incoming = lax.all_to_all(panels[send_list[0, 0]], "cols", 0, 0, tiled=True)
        incoming = incoming.reshape(blocks, tile, rank)
    half = n_rows // 2 if by_hops else 0
    grad, mine, keep_far, give_far, given = rating_part(
        tile_users.reshape(-1), tile_items.reshape(-1), tile_count, target, send_list[0, 0, :, 0], users, items[0],
        ratings[0, 0], similarity[0, 0, :2], own_rows, half,
    )
    if not by_hops:
        contrib = jnp.einsum("kab,kbr->kar", similarity[0, 0], incoming, preferred_element_type=F32)
        flat = grad.reshape(-1, tile, rank).at[target].add(contrib).reshape(icount, rank)
        owned = lax.psum_scatter(flat, "rows", scatter_dimension=0, tiled=True)
        squares = lax.psum(jnp.sum(owned * owned), ("rows", "cols"))
        return (mine.astype(F32) - 0.5 * owned / jnp.sqrt(squares / entries + 1e-06))[None]

    block = jax.ShapeDtypeStruct((half, own_rows, rank), F32)

    def payload(bit):
        return jax.ShapeDtypeStruct((half + len(split_places(half, bit)), own_rows, rank), BF16)

    give = local_call(graph_kernel, "graph_give", (given, give_far, far), block)
    keep = local_call(graph_kernel, "graph_keep", (grad, keep_far, far), block)
    total, sent = local_call(first_kernel, "add_core", (keep, swap(give, "rows", 1)), (block, payload(1)))
    n_hops = len(hops(n_rows, 0))
    for b in range(n_hops - 1):
        total, sent = local_call(
            functools.partial(next_kernel, 1 << b), "add_" + str(b), (total, hop(sent, b)), (block, payload(2 << b))
        )
    own, squares = local_call(
        functools.partial(last_kernel, half // 2), "add_last", (total, hop(sent, n_hops - 1)),
        (jax.ShapeDtypeStruct((own_rows, rank), F32), jax.ShapeDtypeStruct((1, 128), F32)),
    )
    squares = squares + swap(squares, "rows", 1)
    updated = local_call(
        functools.partial(update_kernel, entries), "update", (mine, own, squares, swap(squares, ("rows", "cols"), 3)),
        jax.ShapeDtypeStruct((own_rows, rank), F32),
    )
    return updated[None]


def solution(mesh):
    in_specs = (
        P("rows", None),
        P("cols", None, None),
        P("rows", "cols", None, None, None),
        P("rows", "cols", None),
        P("rows", "cols", None),
        P("rows", "cols"),
        P("rows", "cols", None, None),
        P("rows", "cols", None),
        P("rows", "cols", None, None, None),
    )
    out_specs = P("cols", "rows", None)
    return jax.shard_map(shards, mesh=mesh, in_specs=in_specs, out_specs=out_specs, check_vma=False)
```

```python
import functools

import jax
import jax.numpy as jnp
from jax import lax
from jax.experimental import pallas as pl
from jax.experimental.pallas import tpu as pltpu
from jax.sharding import PartitionSpec as P

F32 = jnp.float32
BF16 = jnp.bfloat16
UNROLL = 8
SMALL = 4 * 1024 * 1024


def in_hbm(*arrays):
    return [pltpu.with_memory_space_constraint(a, pltpu.HBM) for a in arrays]


def dot(a, b, dims):
    return lax.dot_general(a, b, (dims, ((), ())), preferred_element_type=F32)


def rating_kernel(half, user_idx_hbm, item_idx_hbm, target_hbm, count, list_hbm, users, items, ratings, similarity, *refs):
    grad_out, mine_ref, keep_far, give_far, give_out = refs[:5]
    grad_ref, far_ref, user_idx, item_idx, target, send_list, items_t, pred, err, sem_s = refs[5:]
    n_tiles, tile = ratings.shape[0], ratings.shape[1]
    n_item = items.shape[0] // tile
    scalars = [
        pltpu.make_async_copy(source, place, sem_s.at[n])
        for n, (source, place) in enumerate(
            ((target_hbm, target), (list_hbm, send_list), (user_idx_hbm, user_idx), (item_idx_hbm, item_idx))
        )
    ]
    for copy in scalars:
        copy.start()
    own = mine_ref.shape[0]
    mine_ref[...] = items[pl.ds(pl.multiple_of(lax.axis_index("rows") * own, own), own), :]
    for j in range(n_item):
        items_t[j] = items[j * tile:(j + 1) * tile, :].T
    for first in range(0, n_item, 2):
        both = range(first, min(first + 2, n_item))
        whole = dot(users[...], jnp.concatenate([items_t[j] for j in both], axis=1), ((1,), (0,)))
        for n, j in enumerate(both):
            pred[j] = whole[:, n * tile:(n + 1) * tile]

    @pl.loop(0, users.shape[0] // tile)
    def _(c):
        for j in range(n_item):
            err[j, pl.ds(pl.multiple_of(c * tile, tile), tile), :] = jnp.zeros((tile, tile), F32)

    for copy in scalars:
        copy.wait()
    live = count[0, 0]
    col = lax.axis_index("cols")
    block = similarity[1 - col]
    for j in range(n_item):
        far_ref[j * tile:(j + 1) * tile, :] = jnp.where(target[1 - col] == j, block, jnp.zeros_like(block))

    def add_tile(t):
        j = item_idx[t]
        rows = pl.ds(pl.multiple_of(user_idx[t] * tile, tile), tile)
        diff = pred[j, rows, :] - ratings[t].astype(F32)
        err[j, rows, :] += diff.astype(BF16).astype(F32)

    groups = lax.div(live, UNROLL)

    @pl.loop(0, groups)
    def _(g):
        for k in range(UNROLL):
            add_tile(g * UNROLL + k)

    @pl.loop(groups * UNROLL, live)
    def _(t):
        add_tile(t)

    for j in range(n_item):
        whole = err[j]
        high = whole.astype(BF16)
        low = (whole - high.astype(F32)).astype(BF16)
        whole = dot(jnp.concatenate([high, low], axis=1), users[...], ((0,), (0,)))
        grad_ref[j * tile:(j + 1) * tile, :] = whole[:tile] + whole[tile:]
    if not half:
        grad_out[...] = grad_ref[...]
        return
    rows = pl.ds(pl.multiple_of(target[col] * tile, tile), tile)
    near = items[pl.ds(pl.multiple_of(send_list[col] * tile, tile), tile), :]
    grad_ref[rows, :] += dot(similarity[col], near, ((1,), (0,)))
    me = lax.axis_index("rows")
    odd = sum((me >> b) & 1 for b in range(half.bit_length())) % 2
    for q in range(half):
        even_place, odd_place = (offset(2 * half, parity_, q) for parity_ in (0, 1))
        span = slice(q * own, (q + 1) * own)
        for out, far_out, place in (
            (grad_out, keep_far, me ^ jnp.where(odd == 1, odd_place, even_place)),
            (give_out, give_far, me ^ 1 ^ jnp.where(odd == 1, even_place, odd_place)),
        ):
            rows = pl.ds(pl.multiple_of(place * own, own), own)
            out[span, :] = grad_ref[rows, :]
            far_out[span, :] = far_ref[rows, :]


def rating_part(user_idx, item_idx, count, target, send_list, users, items, ratings, similarity, own_rows, half):
    tile = ratings.shape[1]
    n_item = items.shape[0] // tile
    smem = pl.BlockSpec(memory_space=pltpu.SMEM)
    hbm = pl.BlockSpec(memory_space=pltpu.HBM)
    vmem = pl.BlockSpec(memory_space=pltpu.VMEM)
    sums = pltpu.VMEM((n_item, users.shape[0], tile), F32)
    limit = 16 if n_item <= 2 else 56
    count_rows = half * own_rows if half else items.shape[0]
    rows = jax.ShapeDtypeStruct((count_rows, items.shape[1]), F32)
    far_rows = jax.ShapeDtypeStruct((count_rows, tile), BF16)
    return pl.pallas_call(
        functools.partial(rating_kernel, half),
        name="rating_part",
        out_shape=(rows, jax.ShapeDtypeStruct((own_rows, items.shape[1]), BF16), far_rows, far_rows, rows),
        in_specs=[hbm] * 3 + [smem, hbm] + [vmem] * 4,
        out_specs=(vmem,) * 5,
        scratch_shapes=[
            pltpu.VMEM(items.shape, F32),
            pltpu.VMEM((items.shape[0], tile), BF16),
            pltpu.SMEM(user_idx.shape, jnp.int32),
            pltpu.SMEM(item_idx.shape, jnp.int32),
            pltpu.SMEM(target.shape, jnp.int32),
            pltpu.SMEM(send_list.shape, jnp.int32),
            pltpu.VMEM((n_item, items.shape[1], tile), BF16),
            sums,
            sums,
            pltpu.SemaphoreType.DMA((4,)),
        ],
        compiler_params=pltpu.CompilerParams(vmem_limit_bytes=limit * 1024 * 1024),
    )(*in_hbm(user_idx, item_idx, target), count, *in_hbm(send_list), users, items, ratings, similarity)


def pick_kernel(send_list_hbm, items_hbm, sent, send_list, items, sem_s, sems):
    tile = sent.shape[0]
    copy_list = pltpu.make_async_copy(send_list_hbm, send_list, sem_s)
    copies = []
    for n in range(sems.shape[0]):
        rows = pl.ds(n * tile // 2, tile // 2)
        copies.append(pltpu.make_async_copy(items_hbm.at[rows], items.at[rows], sems.at[n]))
    for copy in copies:
        copy.start()
    copy_list.start()
    copy_list.wait()
    for copy in copies:
        copy.wait()
    me = lax.axis_index("cols")
    sent[...] = items[pl.ds(pl.multiple_of(send_list[1 - me] * tile, tile), tile), :]


def pick_panels(send_list, items, tile):
    panel = jax.ShapeDtypeStruct((tile, items.shape[1]), BF16)
    vmem = pl.BlockSpec(memory_space=pltpu.VMEM)
    return pl.pallas_call(
        pick_kernel,
        name="pick_panels",
        out_shape=panel,
        in_specs=[pl.BlockSpec(memory_space=pltpu.HBM)] * 2,
        out_specs=vmem,
        scratch_shapes=[
            pltpu.SMEM(send_list.shape, jnp.int32),
            pltpu.VMEM(items.shape, BF16),
            pltpu.SemaphoreType.DMA,
            pltpu.SemaphoreType.DMA((2 * items.shape[0] // tile,)),
        ],
        compiler_params=pltpu.CompilerParams(vmem_limit_bytes=SMALL),
        cost_estimate=pl.CostEstimate(flops=10**10, bytes_accessed=3 * 10**7, transcendentals=0),
    )(*in_hbm(send_list, items))


def parity(value):
    return bin(value).count("1") % 2


def hops(n_rows, odd):
    bits = [1 << b for b in range(1, n_rows.bit_length() - 1)]
    return bits[1:] + bits[:1] if odd else bits


def offset(n_rows, odd, q):
    value = sum(bit for b, bit in enumerate(hops(n_rows, odd)) if q >> b & 1)
    return value | parity(value)


def graph_kernel(grad, far_blocks, far, total):
    whole = grad[...] + dot(far_blocks[...], far[...], ((1,), (0,)))
    total[...] = whole.reshape(total.shape)


def split_places(half, bit):
    return [q for q in range(half) if q & bit and not q & (bit - 1)]


def pack(total, payload, bit):
    half = total.shape[0]
    for q in range(half):
        payload[q] = total[q].astype(BF16)
    for n, q in enumerate(split_places(half, bit)):
        whole = total[q]
        payload[half + n] = (whole - whole.astype(BF16).astype(F32)).astype(BF16)


def unpack(received, q, bit, half):
    other = q ^ bit
    value = received[other].astype(F32)
    places = split_places(half, bit)
    if other in places:
        value = value + received[half + places.index(other)].astype(F32)
    return value


def first_kernel(keep, received, total, payload):
    total[...] = keep[...] + received[...]
    pack(total, payload, 1)


def next_kernel(bit, before, received, total, payload):
    half = total.shape[0]
    for q in range(half):
        total[q] = before[q] + unpack(received, q, bit, half)
    pack(total, payload, 2 * bit)


def last_kernel(bit, before, received, own, squares):
    half, rows, rank = before.shape
    part = jnp.zeros((8, 128), F32)
    for q in range(half):
        value = before[q] + unpack(received, q, bit, half)
        if q == 0:
            own[...] = value
        square = value * value
        for a in range(0, rows, 8):
            for b in range(0, rank, 128):
                part = part + square[a:a + 8, b:b + 128]
    squares[...] = jnp.sum(part, axis=0, keepdims=True)


def local_call(kernel, name, args, out_shape):
    vmem = pl.BlockSpec(memory_space=pltpu.VMEM)
    return pl.pallas_call(
        kernel, name=name, out_shape=out_shape, in_specs=[vmem] * len(args),
        out_specs=jax.tree.map(lambda unused: vmem, out_shape),
        compiler_params=pltpu.CompilerParams(vmem_limit_bytes=SMALL),
    )(*args)


def update_kernel(entries, mine, own, squares, more, new):
    meansq = jnp.sum(jnp.broadcast_to(squares[...] + more[...], (8, 128)), axis=1, keepdims=True)[:1] * (1 / entries)
    new[...] = mine[...].astype(F32) - own[...] * (0.5 * lax.rsqrt(meansq + 1e-06))


def swap(value, axis, bit):
    size = lax.axis_size(axis)
    return lax.ppermute(value, axis, [(i, i ^ bit) for i in range(size)])


def hop(value, b):
    size = lax.axis_size("rows")
    return lax.ppermute(value, "rows", [(i, i ^ 1 ^ hops(size, parity(i))[b]) for i in range(size)])


def shards(
    users, items, ratings, tile_users, tile_items, tile_count, send_list, block_target, similarity
):
    n_rows, n_cols = lax.axis_size("rows"), lax.axis_size("cols")
    icount, rank = items.shape[1:]
    tile = ratings.shape[-1]
    blocks = similarity.shape[2]
    slots = send_list.shape[3]
    own_rows = icount // n_rows
    target = block_target.reshape(-1)
    entries = n_cols * icount * rank
    by_hops = n_rows >= 4 and not n_rows & (n_rows - 1) and n_cols == 2 and slots == 1 and own_rows % 16 == 0
    if by_hops:
        sent = pick_panels(send_list.reshape(-1), items[0], tile)
        far = swap(sent, "cols", 1)
    else:
        panels = items[0].reshape(-1, tile, rank)
        incoming = lax.all_to_all(panels[send_list[0, 0]], "cols", 0, 0, tiled=True)
        incoming = incoming.reshape(blocks, tile, rank)
    half = n_rows // 2 if by_hops else 0
    grad, mine, keep_far, give_far, given = rating_part(
        tile_users.reshape(-1), tile_items.reshape(-1), tile_count, target, send_list[0, 0, :, 0], users, items[0],
        ratings[0, 0], similarity[0, 0, :2], own_rows, half,
    )
    if not by_hops:
        contrib = jnp.einsum("kab,kbr->kar", similarity[0, 0], incoming, preferred_element_type=F32)
        flat = grad.reshape(-1, tile, rank).at[target].add(contrib).reshape(icount, rank)
        owned = lax.psum_scatter(flat, "rows", scatter_dimension=0, tiled=True)
        squares = lax.psum(jnp.sum(owned * owned), ("rows", "cols"))
        return (mine.astype(F32) - 0.5 * owned / jnp.sqrt(squares / entries + 1e-06))[None]

    block = jax.ShapeDtypeStruct((half, own_rows, rank), F32)

    def payload(bit):
        return jax.ShapeDtypeStruct((half + len(split_places(half, bit)), own_rows, rank), BF16)

    give = local_call(graph_kernel, "graph_give", (given, give_far, far), block)
    keep = local_call(graph_kernel, "graph_keep", (grad, keep_far, far), block)
    total, sent = local_call(first_kernel, "add_core", (keep, swap(give, "rows", 1)), (block, payload(1)))
    n_hops = len(hops(n_rows, 0))
    for b in range(n_hops - 1):
        total, sent = local_call(
            functools.partial(next_kernel, 1 << b), "add_" + str(b), (total, hop(sent, b)), (block, payload(2 << b))
        )
    own, squares = local_call(
        functools.partial(last_kernel, half // 2), "add_last", (total, hop(sent, n_hops - 1)),
        (jax.ShapeDtypeStruct((own_rows, rank), F32), jax.ShapeDtypeStruct((1, 128), F32)),
    )
    squares = squares + swap(squares, ("rows", "cols"), 3)
    updated = local_call(
        functools.partial(update_kernel, entries), "update", (mine, own, squares, swap(squares, "rows", 1)),
        jax.ShapeDtypeStruct((own_rows, rank), F32),
    )
    return updated[None]


def solution(mesh):
    in_specs = (
        P("rows", None),
        P("cols", None, None),
        P("rows", "cols", None, None, None),
        P("rows", "cols", None),
        P("rows", "cols", None),
        P("rows", "cols"),
        P("rows", "cols", None, None),
        P("rows", "cols", None),
        P("rows", "cols", None, None, None),
    )
    out_specs = P("cols", "rows", None)
    return jax.shard_map(shards, mesh=mesh, in_specs=in_specs, out_specs=out_specs, check_vma=False)
```

```python
import functools

import jax
import jax.numpy as jnp
from jax import lax
from jax.experimental import pallas as pl
from jax.experimental.pallas import tpu as pltpu
from jax.sharding import PartitionSpec as P

F32 = jnp.float32
BF16 = jnp.bfloat16
UNROLL = 8
SMALL = 4 * 1024 * 1024


def in_hbm(*arrays):
    return [pltpu.with_memory_space_constraint(a, pltpu.HBM) for a in arrays]


def dot(a, b, dims):
    return lax.dot_general(a, b, (dims, ((), ())), preferred_element_type=F32)


def rating_kernel(half, user_idx_hbm, item_idx_hbm, target_hbm, count, list_hbm, users, items, ratings, similarity, *refs):
    grad_out, mine_ref, keep_far, give_far, give_out = refs[:5]
    grad_ref, far_ref, user_idx, item_idx, target, send_list, items_t, pred, err, sem_s = refs[5:]
    n_tiles, tile = ratings.shape[0], ratings.shape[1]
    n_item = items.shape[0] // tile
    scalars = [
        pltpu.make_async_copy(source, place, sem_s.at[n])
        for n, (source, place) in enumerate(
            ((target_hbm, target), (list_hbm, send_list), (user_idx_hbm, user_idx), (item_idx_hbm, item_idx))
        )
    ]
    for copy in scalars:
        copy.start()
    own = mine_ref.shape[0]
    mine_ref[...] = items[pl.ds(pl.multiple_of(lax.axis_index("rows") * own, own), own), :]
    for j in range(n_item):
        items_t[j] = items[j * tile:(j + 1) * tile, :].T
    for first in range(0, n_item, 2):
        both = range(first, min(first + 2, n_item))
        whole = dot(users[...], jnp.concatenate([items_t[j] for j in both], axis=1), ((1,), (0,)))
        for n, j in enumerate(both):
            pred[j] = whole[:, n * tile:(n + 1) * tile]

    @pl.loop(0, users.shape[0] // tile)
    def _(c):
        for j in range(n_item):
            err[j, pl.ds(pl.multiple_of(c * tile, tile), tile), :] = jnp.zeros((tile, tile), F32)

    for copy in scalars:
        copy.wait()
    live = count[0, 0]
    col = lax.axis_index("cols")
    block = similarity[1 - col]
    for j in range(n_item):
        far_ref[j * tile:(j + 1) * tile, :] = jnp.where(target[1 - col] == j, block, jnp.zeros_like(block))

    def add_tile(t):
        j = item_idx[t]
        rows = pl.ds(pl.multiple_of(user_idx[t] * tile, tile), tile)
        diff = pred[j, rows, :] - ratings[t].astype(F32)
        err[j, rows, :] += diff.astype(BF16).astype(F32)

    groups = lax.div(live, UNROLL)

    @pl.loop(0, groups)
    def _(g):
        for k in range(UNROLL):
            add_tile(g * UNROLL + k)

    @pl.loop(groups * UNROLL, live)
    def _(t):
        add_tile(t)

    for j in range(n_item):
        whole = err[j]
        high = whole.astype(BF16)
        low = (whole - high.astype(F32)).astype(BF16)
        whole = dot(jnp.concatenate([high, low], axis=1), users[...], ((0,), (0,)))
        grad_ref[j * tile:(j + 1) * tile, :] = whole[:tile] + whole[tile:]
    if not half:
        grad_out[...] = grad_ref[...]
        return
    rows = pl.ds(pl.multiple_of(target[col] * tile, tile), tile)
    near = items[pl.ds(pl.multiple_of(send_list[col] * tile, tile), tile), :]
    grad_ref[rows, :] += dot(similarity[col], near, ((1,), (0,)))
    me = lax.axis_index("rows")
    odd = sum((me >> b) & 1 for b in range(half.bit_length())) % 2
    for q in range(half):
        even_place, odd_place = (offset(2 * half, parity_, q) for parity_ in (0, 1))
        span = slice(q * own, (q + 1) * own)
        for out, far_out, place in (
            (grad_out, keep_far, me ^ jnp.where(odd == 1, odd_place, even_place)),
            (give_out, give_far, me ^ 1 ^ jnp.where(odd == 1, even_place, odd_place)),
        ):
            rows = pl.ds(pl.multiple_of(place * own, own), own)
            out[span, :] = grad_ref[rows, :]
            far_out[span, :] = far_ref[rows, :]


def rating_part(user_idx, item_idx, count, target, send_list, users, items, ratings, similarity, own_rows, half):
    tile = ratings.shape[1]
    n_item = items.shape[0] // tile
    smem = pl.BlockSpec(memory_space=pltpu.SMEM)
    hbm = pl.BlockSpec(memory_space=pltpu.HBM)
    vmem = pl.BlockSpec(memory_space=pltpu.VMEM)
    sums = pltpu.VMEM((n_item, users.shape[0], tile), F32)
    limit = 16 if n_item <= 2 else 56
    count_rows = half * own_rows if half else items.shape[0]
    rows = jax.ShapeDtypeStruct((count_rows, items.shape[1]), F32)
    far_rows = jax.ShapeDtypeStruct((count_rows, tile), BF16)
    return pl.pallas_call(
        functools.partial(rating_kernel, half),
        name="rating_part",
        out_shape=(rows, jax.ShapeDtypeStruct((own_rows, items.shape[1]), BF16), far_rows, far_rows, rows),
        in_specs=[hbm] * 3 + [smem, hbm] + [vmem] * 4,
        out_specs=(vmem,) * 5,
        scratch_shapes=[
            pltpu.VMEM(items.shape, F32),
            pltpu.VMEM((items.shape[0], tile), BF16),
            pltpu.SMEM(user_idx.shape, jnp.int32),
            pltpu.SMEM(item_idx.shape, jnp.int32),
            pltpu.SMEM(target.shape, jnp.int32),
            pltpu.SMEM(send_list.shape, jnp.int32),
            pltpu.VMEM((n_item, items.shape[1], tile), BF16),
            sums,
            sums,
            pltpu.SemaphoreType.DMA((4,)),
        ],
        compiler_params=pltpu.CompilerParams(vmem_limit_bytes=limit * 1024 * 1024),
    )(*in_hbm(user_idx, item_idx, target), count, *in_hbm(send_list), users, items, ratings, similarity)


def pick_kernel(send_list_hbm, items_hbm, sent, send_list, items, sem_s, sems):
    tile = sent.shape[0]
    copy_list = pltpu.make_async_copy(send_list_hbm, send_list, sem_s)
    copies = []
    for n in range(sems.shape[0]):
        rows = pl.ds(n * tile // 2, tile // 2)
        copies.append(pltpu.make_async_copy(items_hbm.at[rows], items.at[rows], sems.at[n]))
    for copy in copies:
        copy.start()
    copy_list.start()
    copy_list.wait()
    for copy in copies:
        copy.wait()
    me = lax.axis_index("cols")
    sent[...] = items[pl.ds(pl.multiple_of(send_list[1 - me] * tile, tile), tile), :]


def pick_panels(send_list, items, tile):
    panel = jax.ShapeDtypeStruct((tile, items.shape[1]), BF16)
    vmem = pl.BlockSpec(memory_space=pltpu.VMEM)
    return pl.pallas_call(
        pick_kernel,
        name="pick_panels",
        out_shape=panel,
        in_specs=[pl.BlockSpec(memory_space=pltpu.HBM)] * 2,
        out_specs=vmem,
        scratch_shapes=[
            pltpu.SMEM(send_list.shape, jnp.int32),
            pltpu.VMEM(items.shape, BF16),
            pltpu.SemaphoreType.DMA,
            pltpu.SemaphoreType.DMA((2 * items.shape[0] // tile,)),
        ],
        compiler_params=pltpu.CompilerParams(vmem_limit_bytes=SMALL),
        cost_estimate=pl.CostEstimate(flops=10**10, bytes_accessed=3 * 10**7, transcendentals=0),
    )(*in_hbm(send_list, items))


def parity(value):
    return bin(value).count("1") % 2


def hops(n_rows, odd):
    bits = [1 << b for b in range(1, n_rows.bit_length() - 1)]
    return bits[1::-1] + bits[2:] if odd else bits[:1] + bits[:0:-1]


def offset(n_rows, odd, q):
    value = sum(bit for b, bit in enumerate(hops(n_rows, odd)) if q >> b & 1)
    return value | parity(value)


def graph_kernel(grad, far_blocks, far, total):
    whole = grad[...] + dot(far_blocks[...], far[...], ((1,), (0,)))
    total[...] = whole.reshape(total.shape)


def split_places(half, bit):
    return [q for q in range(half) if q & bit and not q & (bit - 1)]


def pack(total, payload, bit):
    half = total.shape[0]
    for q in range(half):
        payload[q] = total[q].astype(BF16)
    for n, q in enumerate(split_places(half, bit)):
        whole = total[q]
        payload[half + n] = (whole - whole.astype(BF16).astype(F32)).astype(BF16)


def unpack(received, q, bit, half):
    other = q ^ bit
    value = received[other].astype(F32)
    places = split_places(half, bit)
    if other in places:
        value = value + received[half + places.index(other)].astype(F32)
    return value


def first_kernel(keep, received, total, payload):
    total[...] = keep[...] + received[...]
    pack(total, payload, 1)


def next_kernel(bit, before, received, total, payload):
    half = total.shape[0]
    for q in range(half):
        total[q] = before[q] + unpack(received, q, bit, half)
    pack(total, payload, 2 * bit)


def last_kernel(bit, before, received, own, squares):
    half, rows, rank = before.shape
    part = jnp.zeros((8, 128), F32)
    for q in range(half):
        value = before[q] + unpack(received, q, bit, half)
        if q == 0:
            own[...] = value
        square = value * value
        for a in range(0, rows, 8):
            for b in range(0, rank, 128):
                part = part + square[a:a + 8, b:b + 128]
    squares[...] = jnp.sum(part, axis=0, keepdims=True)


def local_call(kernel, name, args, out_shape):
    vmem = pl.BlockSpec(memory_space=pltpu.VMEM)
    return pl.pallas_call(
        kernel, name=name, out_shape=out_shape, in_specs=[vmem] * len(args),
        out_specs=jax.tree.map(lambda unused: vmem, out_shape),
        compiler_params=pltpu.CompilerParams(vmem_limit_bytes=SMALL),
    )(*args)


def update_kernel(entries, mine, own, squares, more, new):
    meansq = jnp.sum(jnp.broadcast_to(squares[...] + more[...], (8, 128)), axis=1, keepdims=True)[:1] * (1 / entries)
    new[...] = mine[...].astype(F32) - own[...] * (0.5 * lax.rsqrt(meansq + 1e-06))


def swap(value, axis, bit):
    size = lax.axis_size(axis)
    return lax.ppermute(value, axis, [(i, i ^ bit) for i in range(size)])


def hop(value, b):
    size = lax.axis_size("rows")
    return lax.ppermute(value, "rows", [(i, i ^ 1 ^ hops(size, parity(i))[b]) for i in range(size)])


def shards(
    users, items, ratings, tile_users, tile_items, tile_count, send_list, block_target, similarity
):
    n_rows, n_cols = lax.axis_size("rows"), lax.axis_size("cols")
    icount, rank = items.shape[1:]
    tile = ratings.shape[-1]
    blocks = similarity.shape[2]
    slots = send_list.shape[3]
    own_rows = icount // n_rows
    target = block_target.reshape(-1)
    entries = n_cols * icount * rank
    by_hops = n_rows >= 4 and not n_rows & (n_rows - 1) and n_cols == 2 and slots == 1 and own_rows % 16 == 0
    if by_hops:
        sent = pick_panels(send_list.reshape(-1), items[0], tile)
        far = swap(sent, "cols", 1)
    else:
        panels = items[0].reshape(-1, tile, rank)
        incoming = lax.all_to_all(panels[send_list[0, 0]], "cols", 0, 0, tiled=True)
        incoming = incoming.reshape(blocks, tile, rank)
    half = n_rows // 2 if by_hops else 0
    grad, mine, keep_far, give_far, given = rating_part(
        tile_users.reshape(-1), tile_items.reshape(-1), tile_count, target, send_list[0, 0, :, 0], users, items[0],
        ratings[0, 0], similarity[0, 0, :2], own_rows, half,
    )
    if not by_hops:
        contrib = jnp.einsum("kab,kbr->kar", similarity[0, 0], incoming, preferred_element_type=F32)
        flat = grad.reshape(-1, tile, rank).at[target].add(contrib).reshape(icount, rank)
        owned = lax.psum_scatter(flat, "rows", scatter_dimension=0, tiled=True)
        squares = lax.psum(jnp.sum(owned * owned), ("rows", "cols"))
        return (mine.astype(F32) - 0.5 * owned / jnp.sqrt(squares / entries + 1e-06))[None]

    block = jax.ShapeDtypeStruct((half, own_rows, rank), F32)

    def payload(bit):
        return jax.ShapeDtypeStruct((half + len(split_places(half, bit)), own_rows, rank), BF16)

    give = local_call(graph_kernel, "graph_give", (given, give_far, far), block)
    keep = local_call(graph_kernel, "graph_keep", (grad, keep_far, far), block)
    total, sent = local_call(first_kernel, "add_core", (keep, swap(give, "rows", 1)), (block, payload(1)))
    n_hops = len(hops(n_rows, 0))
    for b in range(n_hops - 1):
        total, sent = local_call(
            functools.partial(next_kernel, 1 << b), "add_" + str(b), (total, hop(sent, b)), (block, payload(2 << b))
        )
    own, squares = local_call(
        functools.partial(last_kernel, half // 2), "add_last", (total, hop(sent, n_hops - 1)),
        (jax.ShapeDtypeStruct((own_rows, rank), F32), jax.ShapeDtypeStruct((1, 128), F32)),
    )
    squares = squares + swap(squares, "rows", 1)
    updated = local_call(
        functools.partial(update_kernel, entries), "update", (mine, own, squares, swap(squares, ("rows", "cols"), 3)),
        jax.ShapeDtypeStruct((own_rows, rank), F32),
    )
    return updated[None]


def solution(mesh):
    in_specs = (
        P("rows", None),
        P("cols", None, None),
        P("rows", "cols", None, None, None),
        P("rows", "cols", None),
        P("rows", "cols", None),
        P("rows", "cols"),
        P("rows", "cols", None, None),
        P("rows", "cols", None),
        P("rows", "cols", None, None, None),
    )
    out_specs = P("cols", "rows", None)
    return jax.shard_map(shards, mesh=mesh, in_specs=in_specs, out_specs=out_specs, check_vma=False)
```
